256 devices in a mesh: dp: 16 (over z_lo, x), section: 16 (over z_hi, y, core).
Axes of the slice: x: 4, y: 4, z: 8 (z_hi: 2, z_lo: 4; z = z_hi * 4 + z_lo), core: 2. Of those that a mesh axis runs over, the one named last changes fastest.
Arguments:
- act_in: bfloat16 [2, 16, 16, 128, 4608], P(None, 'section', 'dp'), may hold values from -6 to 6
- grad_in: bfloat16 [2, 16, 16, 128, 4608], P(None, 'section', 'dp'), may hold values from -0.125 to 0.125
- saved_inputs: bfloat16 [2, 2, 16, 16, 128, 4608], P(None, None, 'section', 'dp'), may hold values from -6 to 6
- first_key: int32 [16, 128], P('dp'), may hold values from 0 to 127, as said below
- norm_gains: bfloat16 [16, 2, 4608], P('section'), may hold values from 0.5 to 1.5
Outputs:
- act_out: bfloat16 [2, 16, 16, 128, 4608], P(None, 'section', 'dp')
- gain_grad: float32 [16, 2, 4608], P('section')
The draws below stay inside these ranges and needn't reach their ends.
Inputs may be any that keep to these rules, and one draw needn't show every extreme that they name: first_key[r, t] is the first position of the document holding position t of replica r; it never falls along t, first_key[r, 0] = 0, first_key[r, t] <= t, and the last position 127 begins a document of its own in every replica.
All inputs are finite; a program needn't handle non-finite values.
Results may differ from the reference program's by a relative error of at most 0.0056.
Values may be sent and summed in bfloat16 or wider, within the bound.
No kernel may reach another device: no remote copies, remote signals or barrier semaphores. Data moves between devices by JAX's collectives and lax.ppermute only.
A program may use at most 128 MiB of HBM per device.

```python
import jax
import jax.numpy as jnp
from jax import lax

D = 4608
HD = 128
L = 128
ROWS = 16
N_SECTION = 16


def draw_first_key(key, part):
    key = jax.random.fold_in(key, 7)
    positions = lax.broadcasted_iota(jnp.int32, (ROWS, L), 1)
    starts = jax.random.randint(key, (ROWS, L), 0, max(2, L // 8)) == 0
    starts = starts | (positions == L - 1)
    marked = jnp.where(starts, positions, jnp.zeros_like(positions))
    return lax.cummax(marked, axis=1).astype(jnp.int32)


def block_levels(stream_key, shape, split, least, top_value):
    level = 1.0
    for dim, parts in split:
        heights = jax.random.uniform(jax.random.fold_in(jax.random.fold_in(stream_key, 6), dim), (parts,), jnp.float32, least / len(split), top_value / len(split))
        level = level * jnp.repeat(jnp.exp(heights), shape[dim] // parts).reshape((-1,) + (1,) * (len(shape) - 1 - dim))
    return level


def noise(own_key, shape, deviation, bound, pieces=(), held_as=jnp.bfloat16):
    entries = jax.random.normal(own_key, shape, jnp.float32) * deviation
    if len(pieces) > 0:
        entries = block_levels(own_key, shape, pieces, -0.22, 0.18) * entries
    return jnp.clip(entries, min=-bound, max=bound).astype(held_as)


def setup_inputs(seed: int = 0) -> dict:
    key_list = jax.random.split(jax.random.key(seed), 6)
    return {
        "act_in": noise(key_list[0], (2, N_SECTION, ROWS, L, D), 1.0, 6.0, ((1, 16), (2, 16))),
        "grad_in": noise(key_list[1], (2, N_SECTION, ROWS, L, D), 0.02, 0.125, ((1, 16), (2, 16))),
        "saved_inputs": noise(key_list[2], (2, 2, N_SECTION, ROWS, L, D), 1.0, 6.0, ((2, 16), (3, 16))),
        "first_key": draw_first_key(jax.random.fold_in(key_list[5], 71), 0),
        "norm_gains": jnp.clip(1.0 + 0.1 * jax.random.normal(key_list[4], (N_SECTION, 2, D), jnp.float32), 0.5, 1.5).astype(jnp.bfloat16),
    }


epsilon = 1e-06

def visible_mask(first_key):
    seq_len = first_key.shape[0]
    query_pos = lax.broadcasted_iota(jnp.int32, (seq_len, seq_len), 0)
    key_pos = lax.broadcasted_iota(jnp.int32, (seq_len, seq_len), 1)
    return (key_pos <= query_pos) & (key_pos >= first_key[:, None])

def section_parts(hidden, section_gain, first_key):
    seq_len, model_width = hidden.shape
    head_count = model_width // HD
    x_float = hidden.astype(jnp.float32)
    x_scale = lax.rsqrt(lax.optimization_barrier(jnp.mean(x_float * x_float, axis=-1, keepdims=True)) + epsilon)
    normed = lax.optimization_barrier((x_float * x_scale * section_gain[0]).astype(jnp.bfloat16))
    head_float = normed.reshape(seq_len, head_count, HD).astype(jnp.float32)
    scores = jnp.einsum('thc,uhc->htu', head_float, head_float) / HD
    visible = visible_mask(first_key)
    raised = jnp.where(visible[None], jnp.exp(scores), jnp.zeros_like(scores))
    weights = raised / lax.optimization_barrier(jnp.sum(raised, axis=-1, keepdims=True))
    rounded = lax.optimization_barrier(weights.astype(jnp.bfloat16))
    mixed_out = jnp.einsum('htu,uhc->thc', rounded.astype(jnp.float32), head_float).reshape(seq_len, model_width)
    m_scale = lax.rsqrt(lax.optimization_barrier(jnp.mean(mixed_out * mixed_out, axis=-1, keepdims=True)) + epsilon)
    return (x_float, x_scale, head_float, weights, rounded, mixed_out, m_scale)

def section_forward(hidden, section_gain, first_key):
    x_float, x_scale, head_float, weights, rounded, mixed_out, m_scale = section_parts(hidden, section_gain, first_key)
    return (x_float + mixed_out * m_scale * section_gain[1]).astype(jnp.bfloat16)

def section_backward(hidden, section_gain, first_key, cotangent):
    x_float, x_scale, head_float, weights, rounded, mixed_out, m_scale = section_parts(hidden, section_gain, first_key)
    seq_len, model_width = hidden.shape
    head_count = model_width // HD
    dy_float = cotangent.astype(jnp.float32)
    post_grad = section_gain[1] * dy_float
    grad_post = lax.optimization_barrier(jnp.sum(dy_float * mixed_out * m_scale, axis=0))
    d_mixed = m_scale * (post_grad - mixed_out * m_scale * m_scale * lax.optimization_barrier(jnp.mean(post_grad * mixed_out, axis=-1, keepdims=True)))
    d_mixed = lax.optimization_barrier(d_mixed.astype(jnp.bfloat16))
    mixed_float = d_mixed.reshape(seq_len, head_count, HD).astype(jnp.float32)
    d_weights = jnp.einsum('thc,uhc->htu', mixed_float, head_float)
    d_values = jnp.einsum('htu,thc->uhc', rounded.astype(jnp.float32), mixed_float)
    d_scores = weights * (d_weights - lax.optimization_barrier(jnp.sum(weights * d_weights, axis=-1, keepdims=True))) / HD
    d_scores = lax.optimization_barrier(d_scores.astype(jnp.bfloat16)).astype(jnp.float32)
    d_query = jnp.einsum('htu,uhc->thc', d_scores, head_float)
    d_key = jnp.einsum('htu,thc->uhc', d_scores, head_float)
    d_normed = (d_values + d_query + d_key).reshape(seq_len, model_width)
    grad_pre = lax.optimization_barrier(jnp.sum(d_normed * x_float * x_scale, axis=0))
    d_pre = d_normed * section_gain[0]
    d_input = x_scale * (d_pre - x_float * x_scale * x_scale * lax.optimization_barrier(jnp.mean(d_pre * x_float, axis=-1, keepdims=True))) + dy_float
    return (d_input.astype(jnp.bfloat16), jnp.stack([grad_pre, grad_post]))

def reference(act_in, grad_in, saved_inputs, first_key, norm_gains):
    gain_float = norm_gains.astype(jnp.float32)
    section_gains = jnp.stack([gain_float, gain_float[::-1]])
    forward_rows = jax.vmap(section_forward, in_axes=(0, None, 0))
    backward_rows = jax.vmap(section_backward, in_axes=(0, None, 0, 0))

    def forward_all(acts, gains_all):

        def one_section(item):
            return forward_rows(item[0], item[1], first_key)
        return lax.map(one_section, (acts, gains_all))

    def backward_all(inputs_all, gains_all, cotangents):

        def one_section(item):
            return backward_rows(item[0], item[1], first_key, item[2])
        return lax.map(one_section, (inputs_all, gains_all, cotangents))
    once_down = forward_all(act_in[0], section_gains[0])
    once_up = forward_all(act_in[1], section_gains[1])
    zero_block = jnp.zeros_like(once_down[:1])
    received_down = jnp.concatenate([zero_block, once_down[:-1]], axis=0)
    received_up = jnp.concatenate([once_up[1:], zero_block], axis=0)
    out_down = forward_all(received_down, section_gains[0])
    out_up = forward_all(received_up, section_gains[1])
    back_down, first_down = backward_all(saved_inputs[0, 0], section_gains[0], grad_in[0])
    back_up, first_up = backward_all(saved_inputs[1, 0], section_gains[1], grad_in[1])
    arrived_down = jnp.concatenate([back_down[1:], zero_block], axis=0)
    arrived_up = jnp.concatenate([zero_block, back_up[:-1]], axis=0)
    unused_down, second_down = backward_all(saved_inputs[0, 1], section_gains[0], arrived_down)
    unused_up, second_up = backward_all(saved_inputs[1, 1], section_gains[1], arrived_up)
    total_down = lax.optimization_barrier(jnp.sum(first_down + second_down, axis=1))
    total_up = lax.optimization_barrier(jnp.sum(first_up + second_up, axis=1))
    gain_grad = total_down + total_up[::-1]
    return (jnp.stack([out_down, out_up]), gain_grad)
```

```python
import functools

import jax
import jax.numpy as jnp
from jax import lax
from jax.experimental import pallas as pl
from jax.experimental.pallas import tpu as pltpu
from jax.sharding import PartitionSpec as P

HD = 128
EPSILON = 1e-06
LOG2E = 1.4426950408889634
HIDDEN = -1e30
F32 = jnp.float32
BF16 = jnp.bfloat16

NT = (((1,), (1,)), ((), ()))
NN = (((1,), (0,)), ((), ()))


def dot(a, b, dims):
    return lax.dot_general(a, b, dims, preferred_element_type=F32)


def cols(k):
    return slice(k * HD, (k + 1) * HD)


def stages(heads, lag, *steps):
    for i in range(heads + lag * (len(steps) - 1)):
        for place, step in enumerate(steps):
            k = i - lag * place
            if 0 <= k < heads:
                step(k)


def mean_of(total, width):
    return jnp.sum(total, axis=-1, keepdims=True) * (1.0 / width)


def spread(column, rows):
    return jnp.broadcast_to(column, (rows, HD))


def attention(x_ref, gains_ref, pre_row, bias_ref, normed_ref, scores_ref, weights_ref, scale_ref, lag, more):
    rows, width = x_ref.shape
    heads = width // HD
    acc = jnp.zeros((rows, HD), F32)
    for k in range(heads):
        x = x_ref[:, cols(k)].astype(F32)
        acc = acc + x * x
    scale_ref[...] = spread(lax.rsqrt(mean_of(acc, width) + EPSILON), rows)

    def norm(k):
        x = x_ref[:, cols(k)].astype(F32)
        gain = gains_ref[pre_row : pre_row + 1, cols(k)]
        normed_ref[:, cols(k)] = (x * scale_ref[...] * gain).astype(BF16)

    def score(k):
        normed = normed_ref[:, cols(k)]
        scores_ref[:, cols(k)] = dot(normed, normed, NT)

    def soften(k):
        raised = jnp.exp2(scores_ref[:, cols(k)] * (LOG2E / HD) + bias_ref[...])
        total = jnp.sum(raised, axis=-1, keepdims=True)
        weights_ref[:, cols(k)] = (raised * (1.0 / total)).astype(BF16)

    def mix(k):
        scores_ref[:, cols(k)] = dot(weights_ref[:, cols(k)], normed_ref[:, cols(k)], NN)

    stages(heads, lag, norm, score, soften, mix, *more)


def forward_section(x_ref, gains_ref, pre_row, bias_ref, out_ref, normed_ref, weights_ref, mixed_ref, scale_ref, lag):
    rows, width = x_ref.shape
    heads = width // HD
    attention(x_ref, gains_ref, pre_row, bias_ref, normed_ref, mixed_ref, weights_ref, scale_ref, lag, ())
    acc = jnp.zeros((rows, HD), F32)
    for k in range(heads):
        mixed = mixed_ref[:, cols(k)]
        acc = acc + mixed * mixed
    scale_ref[...] = spread(lax.rsqrt(mean_of(acc, width) + EPSILON), rows)
    for k in range(heads):
        x = x_ref[:, cols(k)].astype(F32)
        gain = gains_ref[pre_row + 1 : pre_row + 2, cols(k)]
        out_ref[:, cols(k)] = (x + mixed_ref[:, cols(k)] * scale_ref[...] * gain).astype(BF16)


def forward_kernel(lag, x_ref, gains_ref, bias_ref, out_ref, once_ref, *refs):
    forward_section(x_ref, gains_ref, 0, bias_ref, once_ref, *refs, lag)
    forward_section(once_ref, gains_ref, 2, bias_ref, out_ref, *refs, lag)


def backward_kernel(
    lag,
    with_input,
    x_ref,
    dy_ref,
    gains_ref,
    bias_ref,
    *refs,
):
    if with_input:
        dx_ref, grads_ref, *refs = refs
    else:
        grads_ref, *refs = refs
    normed_ref, weights_ref, mixed_ref, scale_ref, m_ref, b_ref, d_mixed_ref, both_ref, work_ref = refs
    rows, width = x_ref.shape
    heads = width // HD
    attention(x_ref, gains_ref, 0, bias_ref, normed_ref, mixed_ref, weights_ref, scale_ref, lag, ())
    squares = products = jnp.zeros((rows, HD), F32)
    for k in range(heads):
        mixed = mixed_ref[:, cols(k)]
        post_grad = dy_ref[:, cols(k)].astype(F32) * gains_ref[1:2, cols(k)]
        squares = squares + mixed * mixed
        products = products + post_grad * mixed
    m_scale = lax.rsqrt(mean_of(squares, width) + EPSILON)
    m_ref[...] = spread(m_scale, rows)
    b_ref[...] = spread(m_scale * m_scale * m_scale * mean_of(products, width), rows)

    def post(k):
        mixed = mixed_ref[:, cols(k)]
        scaled = dy_ref[:, cols(k)].astype(F32) * m_ref[...]
        grads_ref[1:2, cols(k)] = jnp.sum(scaled * mixed, axis=0, keepdims=True)
        d_mixed_ref[:, cols(k)] = (scaled * gains_ref[1:2, cols(k)] - mixed * b_ref[...]).astype(BF16)

    def weigh(k):
        work_ref[:, cols(k)] = dot(d_mixed_ref[:, cols(k)], normed_ref[:, cols(k)], NT)

    def score(k):
        weights = weights_ref[:, cols(k)].astype(F32)
        d_weights = work_ref[:, cols(k)]
        inner = jnp.sum(weights * d_weights, axis=-1, keepdims=True)
        d_scores = weights * (d_weights - inner) * (1.0 / HD)
        both_ref[:, cols(k)] = (d_scores + d_scores.T).astype(BF16)

    def values(k):
        work_ref[:, cols(k)] = dot(weights_ref[:, cols(k)].T, d_mixed_ref[:, cols(k)], NN) + dot(
            both_ref[:, cols(k)], normed_ref[:, cols(k)], NN
        )

    def pre(k):
        x = x_ref[:, cols(k)].astype(F32)
        grads_ref[0:1, cols(k)] = jnp.sum(work_ref[:, cols(k)] * (x * scale_ref[...]), axis=0, keepdims=True)

    stages(heads, lag, post, weigh, score, values, pre)
    if not with_input:
        return
    products = jnp.zeros((rows, HD), F32)
    for k in range(heads):
        d_pre = work_ref[:, cols(k)] * gains_ref[0:1, cols(k)]
        products = products + d_pre * x_ref[:, cols(k)].astype(F32)
    x_scale = scale_ref[...]
    b_ref[...] = x_scale * x_scale * x_scale * spread(mean_of(products, width), rows)
    for k in range(heads):
        x = x_ref[:, cols(k)].astype(F32)
        dy = dy_ref[:, cols(k)].astype(F32)
        d_pre = work_ref[:, cols(k)] * gains_ref[0:1, cols(k)]
        dx_ref[:, cols(k)] = (scale_ref[...] * d_pre - x * b_ref[...] + dy).astype(BF16)


def whole(count):
    return [pl.BlockSpec(memory_space=pltpu.VMEM)] * count


PARAMS = pltpu.CompilerParams(vmem_limit_bytes=40 * 1024 * 1024)


def forward_twice(x, gains, bias, lag=36):
    rows, width = x.shape
    return pl.pallas_call(
        functools.partial(forward_kernel, lag),
        out_shape=jax.ShapeDtypeStruct((rows, width), BF16),
        in_specs=whole(3),
        out_specs=whole(1)[0],
        scratch_shapes=[
            pltpu.VMEM((rows, width), BF16),
            pltpu.VMEM((rows, width), BF16),
            pltpu.VMEM((rows, width), BF16),
            pltpu.VMEM((rows, width), F32),
            pltpu.VMEM((rows, HD), F32),
        ],
        compiler_params=PARAMS,
        cost_estimate=pl.CostEstimate(flops=8 * rows * rows * width, bytes_accessed=15_000_000, transcendentals=0),
        name="forward_twice",
    )(x, gains, bias)


def backward(x, dy, gains, bias, with_input, lag=36):
    rows, width = x.shape
    grads = jax.ShapeDtypeStruct((2, width), F32)
    dx = jax.ShapeDtypeStruct((rows, width), BF16)
    out_shape = (dx, grads) if with_input else (grads,)
    return pl.pallas_call(
        functools.partial(backward_kernel, lag, with_input),
        out_shape=out_shape,
        in_specs=whole(4),
        out_specs=tuple(whole(len(out_shape))),
        scratch_shapes=[
            pltpu.VMEM((rows, width), BF16),
            pltpu.VMEM((rows, width), BF16),
            pltpu.VMEM((rows, width), F32),
            pltpu.VMEM((rows, HD), F32),
            pltpu.VMEM((rows, HD), F32),
            pltpu.VMEM((rows, HD), F32),
            pltpu.VMEM((rows, width), BF16),
            pltpu.VMEM((rows, width), BF16),
            pltpu.VMEM((rows, width), F32),
        ],
        compiler_params=PARAMS,
        cost_estimate=pl.CostEstimate(flops=12 * rows * rows * width, bytes_accessed=20_000_000, transcendentals=0),
        name="backward",
    )(x, dy, gains, bias)


def moved(block, shift):
    count = lax.axis_size("section")
    pairs = [(i, i + shift) for i in range(count) if 0 <= i + shift < count]
    return lax.ppermute(block, "section", pairs)


def reflected(block, top):
    count = lax.axis_size("section")
    pairs = [(i, top - i) for i in range(count) if 0 <= top - i < count]
    return lax.ppermute(block, "section", pairs)


def summed_over_replicas(value):
    count = lax.axis_size("dp")
    stride = 1
    while stride < count:
        size = 4 if count % (stride * 4) == 0 else count // stride
        total = value
        for step in range(1, size):
            pairs = []
            for i in range(count):
                place = i // stride % size
                pairs.append((i, i + ((place + step) % size - place) * stride))
            total = total + lax.ppermute(value, "dp", pairs)
        value = total
        stride *= size
    return value


def body(act_in, grad_in, saved_inputs, first_key, norm_gains):
    rows = act_in.shape[3]
    top = lax.axis_size("section") - 1
    own = norm_gains[0]
    mirrored = reflected(own, top)
    behind = moved(own, 1)
    ahead = reflected(own, top - 1)
    came_saved = (moved(saved_inputs[0, 1, 0, 0], 1), moved(saved_inputs[1, 1, 0, 0], -1))
    came_act = (moved(act_in[0, 0, 0], 1), moved(act_in[1, 0, 0], -1))
    query = lax.broadcasted_iota(jnp.int32, (rows, rows), 0)
    key = lax.broadcasted_iota(jnp.int32, (rows, rows), 1)
    visible = (key <= query) & (key >= first_key[0][:, None])
    bias = jnp.where(visible, 0.0, HIDDEN).astype(F32)
    own, mirrored, behind, ahead = (g.astype(F32) for g in (own, mirrored, behind, ahead))
    back_down, first_down = backward(saved_inputs[0, 0, 0, 0], grad_in[0, 0, 0], own, bias, True)
    back_up, first_up = backward(saved_inputs[1, 0, 0, 0], grad_in[1, 0, 0], mirrored, bias, True)
    (second_down,) = backward(came_saved[0], back_down, behind, bias, False)
    (second_up,) = backward(came_saved[1], back_up, ahead, bias, False)
    total = first_down + reflected(first_up, top)
    total = total + moved(second_down, -1) + reflected(second_up, top - 1)
    combined = summed_over_replicas(total)
    out_down = forward_twice(came_act[0], jnp.concatenate([behind, own]), bias)
    out_up = forward_twice(came_act[1], jnp.concatenate([ahead, mirrored]), bias)
    outputs = jnp.stack([out_down, out_up])[:, None, None]
    return (outputs, combined[None])


def solution(mesh):
    placed = (
        P(None, "section", "dp", None, None),
        P(None, "section", "dp", None, None),
        P(None, None, "section", "dp", None, None),
        P("dp", None),
        P("section", None, None),
    )
    return jax.shard_map(
        body,
        mesh=mesh,
        in_specs=placed,
        out_specs=(P(None, "section", "dp", None, None), P("section", None, None)),
        check_vma=False,
    )
```

```python
import functools

import jax
import jax.numpy as jnp
from jax import lax
from jax.experimental import pallas as pl
from jax.experimental.pallas import tpu as pltpu
from jax.sharding import PartitionSpec as P

HD = 128
EPSILON = 1e-06
LOG2E = 1.4426950408889634
HIDDEN = -1e30
PIECES = 4
COST = 200_000
MEBI = 1024 * 1024
FULL = 60 * MEBI
MOST = 48 * MEBI
PART = 30 * MEBI
TAIL = 16
F32 = jnp.float32
BF16 = jnp.bfloat16

NT = (((1,), (1,)), ((), ()))
NN = (((1,), (0,)), ((), ()))


def dot(a, b, dims):
    return lax.dot_general(a, b, dims, preferred_element_type=F32)


def cols(k):
    return slice(k * HD, (k + 1) * HD)


def mean_of(total, width):
    return jnp.sum(total, axis=-1, keepdims=True) * (1.0 / width)


def spread(column, rows):
    return jnp.broadcast_to(column, (rows, HD))


def pieces(heads):
    step = -(-heads // PIECES)
    return [(low, min(low + step, heads)) for low in range(0, heads, step)]


def copies(source, target, sems, first=0):
    heads = target.shape[1] // HD
    parts = [slice(low * HD, high * HD) for low, high in pieces(heads)]
    return [
        pltpu.make_async_copy(source.at[:, part], target.at[:, part], sems.at[first + i]) for i, part in enumerate(parts)
    ]


def start_all(moves):
    for move in moves:
        move.start()


def wait_all(moves):
    for move in moves:
        move.wait()


def attention(x_ref, waits, gain_of, bias_ref, normed_ref, scores_ref, weights_ref, scale_ref):
    rows, width = x_ref.shape
    heads = width // HD
    acc = jnp.zeros((rows, HD), F32)
    for i, (low, high) in enumerate(pieces(heads)):
        if waits:
            waits[i].wait()
        for k in range(low, high):
            x = x_ref[:, cols(k)].astype(F32)
            acc = acc + x * x
    scale_ref[...] = spread(lax.rsqrt(mean_of(acc, width) + EPSILON), rows)
    for k in range(heads):
        x = x_ref[:, cols(k)].astype(F32)
        normed_ref[:, cols(k)] = (x * scale_ref[...] * gain_of(0, k)).astype(BF16)
    for k in range(heads):
        normed = normed_ref[:, cols(k)]
        scores_ref[:, cols(k)] = dot(normed, normed, NT)
    for k in range(heads):
        raised = jnp.exp2(scores_ref[:, cols(k)] * (LOG2E / HD) + bias_ref[...])
        total = jnp.sum(raised, axis=-1, keepdims=True)
        weights_ref[:, cols(k)] = (raised * (1.0 / total)).astype(BF16)
    for k in range(heads):
        scores_ref[:, cols(k)] = dot(weights_ref[:, cols(k)], normed_ref[:, cols(k)], NN)


def forward_section(x_ref, waits, gain_of, bias_ref, out_ref, normed_ref, weights_ref, mixed_ref, scale_ref):
    rows, width = x_ref.shape
    heads = width // HD
    attention(x_ref, waits, gain_of, bias_ref, normed_ref, mixed_ref, weights_ref, scale_ref)
    acc = jnp.zeros((rows, HD), F32)
    for k in range(heads):
        mixed = mixed_ref[:, cols(k)]
        acc = acc + mixed * mixed
    scale_ref[...] = spread(lax.rsqrt(mean_of(acc, width) + EPSILON), rows)
    for k in range(heads):
        x = x_ref[:, cols(k)].astype(F32)
        out_ref[:, cols(k)] = (x + mixed_ref[:, cols(k)] * scale_ref[...] * gain_of(1, k)).astype(BF16)


def backward_section(x_ref, waits, wait_dy, dy_ref, gain_of, bias_ref, dx_ref, grads_ref, refs):
    normed_ref, weights_ref, mixed_ref, scale_ref, m_ref, b_ref, d_mixed_ref, both_ref, work_ref = refs
    rows, width = x_ref.shape
    heads = width // HD
    attention(x_ref, waits, gain_of, bias_ref, normed_ref, mixed_ref, weights_ref, scale_ref)
    wait_dy.wait()
    squares = products = jnp.zeros((rows, HD), F32)
    for k in range(heads):
        mixed = mixed_ref[:, cols(k)]
        post_grad = dy_ref[:, cols(k)].astype(F32) * gain_of(1, k)
        squares = squares + mixed * mixed
        products = products + post_grad * mixed
    m_scale = lax.rsqrt(mean_of(squares, width) + EPSILON)
    m_ref[...] = spread(m_scale, rows)
    b_ref[...] = spread(m_scale * m_scale * m_scale * mean_of(products, width), rows)
    for k in range(heads):
        mixed = mixed_ref[:, cols(k)]
        scaled = dy_ref[:, cols(k)].astype(F32) * m_ref[...]
        grads_ref[1:2, cols(k)] = jnp.sum(scaled * mixed, axis=0, keepdims=True)
        d_mixed_ref[:, cols(k)] = (scaled * gain_of(1, k) - mixed * b_ref[...]).astype(BF16)
    for k in range(heads):
        work_ref[:, cols(k)] = dot(d_mixed_ref[:, cols(k)], normed_ref[:, cols(k)], NT)
    for k in range(heads):
        weights = weights_ref[:, cols(k)].astype(F32)
        d_weights = work_ref[:, cols(k)]
        inner = jnp.sum(weights * d_weights, axis=-1, keepdims=True)
        d_scores = weights * (d_weights - inner) * (1.0 / HD)
        both_ref[:, cols(k)] = (d_scores + d_scores.T).astype(BF16)
    for k in range(heads):
        work_ref[:, cols(k)] = dot(weights_ref[:, cols(k)].T, d_mixed_ref[:, cols(k)], NN) + dot(
            both_ref[:, cols(k)], normed_ref[:, cols(k)], NN
        )
    for k in range(heads):
        x = x_ref[:, cols(k)].astype(F32)
        grads_ref[0:1, cols(k)] = jnp.sum(work_ref[:, cols(k)] * (x * scale_ref[...]), axis=0, keepdims=True)
    if dx_ref is None:
        return
    products = jnp.zeros((rows, HD), F32)
    for k in range(heads):
        d_pre = work_ref[:, cols(k)] * gain_of(0, k)
        products = products + d_pre * x_ref[:, cols(k)].astype(F32)
    x_scale = scale_ref[...]
    b_ref[...] = x_scale * x_scale * x_scale * spread(mean_of(products, width), rows)
    for k in range(heads):
        x = x_ref[:, cols(k)].astype(F32)
        dy = dy_ref[:, cols(k)].astype(F32)
        d_pre = work_ref[:, cols(k)] * gain_of(0, k)
        dx_ref[:, cols(k)] = (scale_ref[...] * d_pre - x * b_ref[...] + dy).astype(BF16)


def gains_in(ref, relay=None):
    if relay is None:
        return lambda which, k: ref[which : which + 1, cols(k)]
    return lambda which, k: ref[relay, which : which + 1, cols(k)]


def arrive(x, dy, x_ref, dy_ref, gains_hbm, gains_ref, bias_hbm, bias_ref, sems):
    loads = copies(x, x_ref, sems) if x is not None else []
    small = [
        pltpu.make_async_copy(gains_hbm, gains_ref, sems.at[PIECES]),
        pltpu.make_async_copy(bias_hbm, bias_ref, sems.at[PIECES + 1]),
    ]
    start_all(loads)
    start_all(small)
    load_dy = None
    if dy is not None:
        load_dy = pltpu.make_async_copy(dy, dy_ref, sems.at[PIECES + 2])
        load_dy.start()
    wait_all(small)
    return loads, load_dy


def pick_kernel(relay_ref, saved_hbm, act_hbm, after, saved_out, act_out, saved_ref, act_ref, sems):
    relay = relay_ref[0]
    rows, width = act_ref.shape
    loads = [
        pltpu.make_async_copy(saved_hbm.at[relay, 1, 0, 0], saved_ref.at[:rows], sems.at[0]),
        pltpu.make_async_copy(act_hbm.at[relay, 0, 0], act_ref, sems.at[1]),
    ]
    stores = [
        pltpu.make_async_copy(saved_ref, saved_out, sems.at[2]),
        pltpu.make_async_copy(act_ref, act_out, sems.at[3]),
    ]
    start_all(loads)
    if saved_ref.shape[0] > rows:
        saved_ref[rows:] = jnp.zeros((saved_ref.shape[0] - rows, width), BF16)
    for load, store in zip(loads, stores):
        load.wait()
        store.start()
    wait_all(stores)


def look_kernel(far_hbm, first_hbm, out_ref, sems):
    look = pltpu.make_async_copy(first_hbm, out_ref, sems.at[0])
    look.start()
    look.wait()


def backward_first_kernel(
    x_hbm, dy_hbm, own_hbm, mirrored_hbm, bias_hbm, way_hbm, dx_down, dx_up, down_ref, up_ref, way_out, all_gains,
    own_ref, mirrored_ref, way_ref, x_up, dy_up, up_gains_ref, up_sems, x_ref, dy_ref, gains_ref, bias_ref, sems, *refs
):
    loads, load_dy = arrive(
        x_hbm.at[0, 0, 0, 0], dy_hbm.at[0, 0, 0], x_ref, dy_ref, own_hbm, own_ref, bias_hbm, bias_ref, sems
    )
    gains_ref[...] = own_ref[...].astype(F32)
    more = [
        pltpu.make_async_copy(x_hbm.at[1, 0, 0, 0], x_up, up_sems.at[0]),
        pltpu.make_async_copy(dy_hbm.at[1, 0, 0], dy_up, up_sems.at[1]),
        pltpu.make_async_copy(mirrored_hbm, mirrored_ref, up_sems.at[2]),
    ]
    pass_way = pltpu.make_async_copy(way_hbm, way_ref, up_sems.at[3])
    start_all(more)
    pass_way.start()
    backward_section(x_ref, loads, load_dy, dy_ref, gains_in(gains_ref), bias_ref, dx_down, down_ref, refs)
    wait_all(more[::2])
    up_gains_ref[...] = mirrored_ref[...].astype(F32)
    all_gains[0] = gains_ref[...]
    all_gains[1] = up_gains_ref[...]
    pass_way.wait()
    store_way = pltpu.make_async_copy(way_ref, way_out, up_sems.at[4])
    store_way.start()
    backward_section(x_up, [], more[1], dy_up, gains_in(up_gains_ref), bias_ref, dx_up, up_ref, refs)
    store_way.wait()


def backward_next_kernel(
    choice_ref, x_hbm, gains_hbm, first_hbm, second_hbm, bias_hbm, after, also, grads_ref,
    tail_ref, x_ref, dy_ref, gains_ref, bias_ref, sems, *refs
):
    rows = x_ref.shape[0]
    loads = copies(x_hbm.at[:rows], x_ref, sems)
    load_dy = pltpu.make_async_copy(first_hbm, dy_ref, sems.at[PIECES + 2])
    load_other = pltpu.make_async_copy(second_hbm, dy_ref, sems.at[PIECES + 2])
    start_all(loads)

    @pl.when(choice_ref[0] == 0)
    def _():
        load_dy.start()

    @pl.when(choice_ref[0] == 1)
    def _():
        load_other.start()

    arrive(None, None, x_ref, None, gains_hbm, tail_ref, bias_hbm, bias_ref, sems)
    gains_ref[...] = tail_ref[...].astype(F32)
    backward_section(x_ref, loads, load_dy, dy_ref, gains_in(gains_ref), bias_ref, None, grads_ref, refs)


def forward_near_kernel(
    relay_ref, act_hbm, tail_hbm, gains_hbm, bias_hbm, early_hbm, out_ref, early_ref,
    tail_ref, tail_gains_ref, once_ref, x_ref, gains_ref, bias_ref, sems, *refs
):
    relay = relay_ref[0]
    load_early = pltpu.make_async_copy(early_hbm, early_ref, sems.at[PIECES + 4])
    load_tail = pltpu.make_async_copy(tail_hbm, tail_ref, sems.at[PIECES + 3])
    load_early.start()
    load_tail.start()
    loads, _ = arrive(
        act_hbm, None, x_ref, None, gains_hbm.at[relay], gains_ref, bias_hbm, bias_ref, sems
    )
    load_tail.wait()
    tail_gains_ref[...] = tail_ref[...].astype(F32)
    forward_section(x_ref, loads, gains_in(tail_gains_ref), bias_ref, once_ref, *refs)
    forward_section(once_ref, [], gains_in(gains_ref), bias_ref, out_ref, *refs)
    load_early.wait()


def forward_once_kernel(
    by_way_ref, direct_hbm, passed_hbm, far_gains_hbm, bias_hbm, early_hbm, after, out_ref, early_ref, tail_ref, x_ref,
    gains_ref, bias_ref, sems, *refs
):
    load_early = pltpu.make_async_copy(early_hbm, early_ref, sems.at[PIECES + 3])
    load_early.start()
    direct = copies(direct_hbm, x_ref, sems)
    passed = copies(passed_hbm, x_ref, sems)

    @pl.when(by_way_ref[0] == 1)
    def _():
        start_all(passed)

    @pl.when(by_way_ref[0] == 0)
    def _():
        start_all(direct)

    arrive(None, None, x_ref, None, far_gains_hbm, tail_ref, bias_hbm, bias_ref, sems)
    gains_ref[...] = tail_ref[...].astype(F32)
    forward_section(x_ref, direct, gains_in(gains_ref), bias_ref, out_ref, *refs)
    load_early.wait()


def forward_far_kernel(
    relay_ref, x_hbm, gains_hbm, bias_hbm, near_hbm, early_hbm, out_ref, early_ref, x_ref, gains_ref, bias_ref, sems, *refs
):
    relay = relay_ref[0]
    load_early = pltpu.make_async_copy(early_hbm, early_ref, sems.at[PIECES + 2])
    load_near = pltpu.make_async_copy(near_hbm, out_ref.at[1 - relay, 0, 0], sems.at[PIECES + 3])
    load_early.start()
    load_near.start()
    loads, _ = arrive(x_hbm, None, x_ref, None, gains_hbm.at[relay], gains_ref, bias_hbm, bias_ref, sems)
    forward_section(x_ref, loads, gains_in(gains_ref), bias_ref, out_ref.at[relay, 0, 0], *refs)
    load_near.wait()
    load_early.wait()


SMALL = pl.BlockSpec(memory_space=pltpu.SMEM)
NEAR = pl.BlockSpec(memory_space=pltpu.VMEM)
FAR = pl.BlockSpec(memory_space=pl.ANY)
PLAIN = pl.BlockSpec(memory_space=pltpu.HBM)


def call(kernel, name, operands, out_specs, out_shape, held, rows, width, kind, vmem=PART):
    block = pltpu.VMEM((rows, width), BF16)
    scratch = [block if h is None else h for h in held]
    if kind > 0:
        scratch += [
            pltpu.VMEM((2, width), F32),
            pltpu.VMEM((rows, rows), F32),
            pltpu.SemaphoreType.DMA((PIECES + 5,)),
            block,
            block,
            pltpu.VMEM((rows, width), F32),
            pltpu.VMEM((rows, HD), F32),
        ]
    if kind > 1:
        scratch += [pltpu.VMEM((rows, HD), F32), pltpu.VMEM((rows, HD), F32), block, block, pltpu.VMEM((rows, width), F32)]
    return pl.pallas_call(
        kernel,
        out_shape=out_shape,
        in_specs=[SMALL if x.dtype == jnp.int32 else PLAIN if x.ndim > 4 else FAR for x in operands],
        out_specs=out_specs,
        scratch_shapes=scratch,
        compiler_params=pltpu.CompilerParams(vmem_limit_bytes=vmem),
        cost_estimate=pl.CostEstimate(flops=0, bytes_accessed=COST, transcendentals=0),
        name=name,
    )(*operands)


def shape(*sizes, dtype=BF16):
    return jax.ShapeDtypeStruct(sizes, dtype)


def pick(relay, saved, act, after, tail):
    rows, width = act.shape[-2:]
    return call(
        pick_kernel, "pick", (relay, saved, act, after), (FAR, FAR), (shape(rows + tail, width), shape(rows, width)),
        [pltpu.VMEM((rows + tail, width), BF16), None, pltpu.SemaphoreType.DMA((4,))], rows, width, 0, FULL,
    )


def look(far, first):
    rows, width = far.shape
    return call(
        look_kernel, "look", (far, first), NEAR, shape(*first.shape, dtype=F32), [pltpu.SemaphoreType.DMA((1,))],
        rows, width, 0,
    )


def backward_first(x, dy, own, mirrored, bias, way):
    rows, width = way.shape
    block = shape(rows, width)
    held = shape(2, width, dtype=F32)
    small = pltpu.VMEM((2, width), BF16)
    return call(
        backward_first_kernel, "backward_first", (x, dy, own, mirrored, bias, way), (NEAR,) * 4 + (FAR, NEAR),
        (block, block, held, held, block, shape(2, 2, width, dtype=F32)),
        [small, small, None, None, None, pltpu.VMEM((2, width), F32), pltpu.SemaphoreType.DMA((5,)), None, None],
        rows, width, 2, MOST,
    )


def backward_next(choice, x, gains, first, second, bias, after, also):
    rows, width = first.shape
    return call(
        backward_next_kernel, "backward_next", (choice, x, gains, first, second, bias, after, also),
        NEAR, shape(2, width, dtype=F32), [pltpu.VMEM((2, width), BF16), None, None], rows, width, 2,
    )


def forward_near(relay, act, tail, gains, bias, early):
    rows, width = act.shape
    return call(
        forward_near_kernel, "forward_near", (relay, act, tail, gains, bias, early), (NEAR, NEAR),
        (shape(rows, width), shape(*early.shape, dtype=F32)),
        [pltpu.VMEM((2, width), BF16), pltpu.VMEM((2, width), F32), None, None], rows, width, 1,
    )


def forward_once(by_way, direct, passed, far_gains, bias, early, after):
    rows, width = direct.shape
    return call(
        forward_once_kernel, "forward_once", (by_way, direct, passed, far_gains, bias, early, after), (NEAR, NEAR),
        (shape(rows, width), shape(*early.shape, dtype=F32)), [pltpu.VMEM((2, width), BF16), None], rows, width, 1,
    )


def forward_far(relay, x, gains, bias, near, early):
    rows, width = x.shape
    return call(
        forward_far_kernel, "forward_far", (relay, x, gains, bias, near, early), (NEAR, NEAR),
        (shape(2, 1, 1, rows, width), shape(*early.shape, dtype=F32)), [None], rows, width, 1,
    )


def summed_along(value, total, axis, stride, size):
    for step in range(1, size):
        pairs = []
        for i in range(lax.axis_size(axis)):
            place = i // stride % size
            pairs.append((i, i + ((place + step) % size - place) * stride))
        total = total + lax.ppermute(value, axis, pairs)
    return total


def routes(count):
    low, high, last = count // 2 - 1, count // 2, count - 1
    near = [(i, i ^ 1) for i in range(count)]
    far = [(i, i + 1) for i in range(1, last, 2) if i != low]
    far = far + [(b, a) for a, b in far]
    straight = [(low, high), (high, low)]
    out = [(low, 0), (high, last)]
    on = [(0, high), (last, low)]
    return near, far, straight, out, on


def body(act_in, grad_in, saved_inputs, first_key, norm_gains):
    rows = act_in.shape[3]
    count = lax.axis_size("section")
    last = count - 1
    near, far, straight, out, on = routes(count)
    mirror = [(i, last - i) for i in range(count)]
    section = lax.axis_index("section")
    odd = section % 2
    ends = (section == count // 2 - 1) | (section == count // 2)
    outer = jnp.stack([1 - odd]).astype(jnp.int32)
    inner = jnp.stack([odd]).astype(jnp.int32)
    by_way = jnp.stack([ends]).astype(jnp.int32)

    own = norm_gains[0]
    mirrored = lax.ppermute(own, "section", mirror)
    query = lax.broadcasted_iota(jnp.int32, (rows, rows), 0)
    key = lax.broadcasted_iota(jnp.int32, (rows, rows), 1)
    visible = (key <= query) & (key >= first_key[0][:, None])
    bias = jnp.where(visible, 0.0, HIDDEN).astype(F32)
    far_sent, act_sent = pick(outer, saved_inputs, act_in, bias, TAIL)
    near_sent, near_act = pick(inner, saved_inputs, act_in, mirrored, TAIL)
    far_block = lax.ppermute(far_sent, "section", far + straight)
    half_way = lax.ppermute(act_sent, "section", out)
    far_act = lax.ppermute(act_sent, "section", far)
    near_block = lax.ppermute(near_sent, "section", near)
    near_act = lax.ppermute(near_act, "section", near)
    far_gains = lax.ppermute(jnp.where(odd == 1, own, mirrored), "section", far + straight)
    near_gains = lax.ppermute(jnp.where(odd == 1, mirrored, own), "section", near)

    dx_down, dx_up, first_down, first_up, half_way, gains = backward_first(
        saved_inputs, grad_in, own, mirrored, bias, half_way
    )
    passed_act = lax.ppermute(half_way, "section", on)
    near_out, first_up = forward_near(outer, near_act, near_gains, gains, bias, first_up)
    first_up = look(far_block, first_up)
    far_second = backward_next(inner, far_block, far_gains, dx_down, dx_up, bias, first_up, first_up)
    near_second = backward_next(inner, near_block, near_gains, dx_up, dx_down, bias, far_second, far_act)
    there = lax.ppermute(first_up, "section", mirror)
    down = jnp.where(odd == 1, near_second, far_second)
    up = jnp.where(odd == 1, far_second, near_second)
    down = lax.ppermute(down, "section", [(i, i - 1) for i in range(1, count)])
    up = lax.ppermute(up, "section", [(i, last - 1 - i) for i in range(last)])
    once, here = forward_once(by_way, far_act, passed_act, far_gains, bias, first_down, near_second)
    total = here + there + down + up
    outputs, same = forward_far(inner, once, gains, bias, near_out, total)
    part = summed_along(total, same, "dp", 1, 4)
    combined = summed_along(part, part, "dp", 4, lax.axis_size("dp") // 4)
    return (outputs, combined[None])


def solution(mesh):
    placed = (
        P(None, "section", "dp", None, None),
        P(None, "section", "dp", None, None),
        P(None, None, "section", "dp", None, None),
        P("dp", None),
        P("section", None, None),
    )
    return jax.shard_map(
        body,
        mesh=mesh,
        in_specs=placed,
        out_specs=(P(None, "section", "dp", None, None), P("section", None, None)),
        check_vma=False,
    )
```

```python
import functools

import jax
import jax.numpy as jnp
from jax import lax
from jax.experimental import pallas as pl
from jax.experimental.pallas import tpu as pltpu
from jax.sharding import PartitionSpec as P

HD = 128
EPSILON = 1e-06
LOG2E = 1.4426950408889634
HIDDEN = -1e30
PIECES = 4
COST = 200_000
MEBI = 1024 * 1024
FULL = 60 * MEBI
MOST = 48 * MEBI
PART = 30 * MEBI
TAIL = 16
F32 = jnp.float32
BF16 = jnp.bfloat16

NT = (((1,), (1,)), ((), ()))
NN = (((1,), (0,)), ((), ()))


def dot(a, b, dims):
    return lax.dot_general(a, b, dims, preferred_element_type=F32)


def cols(k):
    return slice(k * HD, (k + 1) * HD)


def mean_of(total, width):
    return jnp.sum(total, axis=-1, keepdims=True) * (1.0 / width)


def spread(column, rows):
    return jnp.broadcast_to(column, (rows, HD))


def pieces(heads):
    step = -(-heads // PIECES)
    return [(low, min(low + step, heads)) for low in range(0, heads, step)]


def copies(source, target, sems, first=0):
    heads = target.shape[1] // HD
    parts = [slice(low * HD, high * HD) for low, high in pieces(heads)]
    return [
        pltpu.make_async_copy(source.at[:, part], target.at[:, part], sems.at[first + i]) for i, part in enumerate(parts)
    ]


def start_all(moves):
    for move in moves:
        move.start()


def wait_all(moves):
    for move in moves:
        move.wait()


def attention(x_ref, waits, gain_of, bias_ref, normed_ref, scores_ref, weights_ref, scale_ref):
    rows, width = x_ref.shape
    heads = width // HD
    acc = jnp.zeros((rows, HD), F32)
    for i, (low, high) in enumerate(pieces(heads)):
        if waits:
            waits[i].wait()
        for k in range(low, high):
            x = x_ref[:, cols(k)].astype(F32)
            acc = acc + x * x
    scale_ref[...] = spread(lax.rsqrt(mean_of(acc, width) + EPSILON), rows)
    for k in range(heads):
        x = x_ref[:, cols(k)].astype(F32)
        normed_ref[:, cols(k)] = (x * scale_ref[...] * gain_of(0, k)).astype(BF16)
    for k in range(heads):
        normed = normed_ref[:, cols(k)]
        scores_ref[:, cols(k)] = dot(normed, normed, NT)
    for k in range(heads):
        raised = jnp.exp2(scores_ref[:, cols(k)] * (LOG2E / HD) + bias_ref[...])
        total = jnp.sum(raised, axis=-1, keepdims=True)
        weights_ref[:, cols(k)] = (raised * (1.0 / total)).astype(BF16)
    for k in range(heads):
        scores_ref[:, cols(k)] = dot(weights_ref[:, cols(k)], normed_ref[:, cols(k)], NN)


def forward_section(x_ref, waits, gain_of, bias_ref, out_ref, normed_ref, weights_ref, mixed_ref, scale_ref):
    rows, width = x_ref.shape
    heads = width // HD
    attention(x_ref, waits, gain_of, bias_ref, normed_ref, mixed_ref, weights_ref, scale_ref)
    acc = jnp.zeros((rows, HD), F32)
    for k in range(heads):
        mixed = mixed_ref[:, cols(k)]
        acc = acc + mixed * mixed
    scale_ref[...] = spread(lax.rsqrt(mean_of(acc, width) + EPSILON), rows)
    for k in range(heads):
        x = x_ref[:, cols(k)].astype(F32)
        out_ref[:, cols(k)] = (x + mixed_ref[:, cols(k)] * scale_ref[...] * gain_of(1, k)).astype(BF16)


def backward_section(x_ref, waits, wait_dy, dy_ref, gain_of, bias_ref, dx_ref, grads_ref, refs):
    normed_ref, weights_ref, mixed_ref, scale_ref, m_ref, b_ref, d_mixed_ref, both_ref, work_ref = refs
    rows, width = x_ref.shape
    heads = width // HD
    attention(x_ref, waits, gain_of, bias_ref, normed_ref, mixed_ref, weights_ref, scale_ref)
    wait_dy.wait()
    squares = products = jnp.zeros((rows, HD), F32)
    for k in range(heads):
        mixed = mixed_ref[:, cols(k)]
        post_grad = dy_ref[:, cols(k)].astype(F32) * gain_of(1, k)
        squares = squares + mixed * mixed
        products = products + post_grad * mixed
    m_scale = lax.rsqrt(mean_of(squares, width) + EPSILON)
    m_ref[...] = spread(m_scale, rows)
    b_ref[...] = spread(m_scale * m_scale * m_scale * mean_of(products, width), rows)
    for k in range(heads):
        mixed = mixed_ref[:, cols(k)]
        scaled = dy_ref[:, cols(k)].astype(F32) * m_ref[...]
        grads_ref[1:2, cols(k)] = jnp.sum(scaled * mixed, axis=0, keepdims=True)
        d_mixed_ref[:, cols(k)] = (scaled * gain_of(1, k) - mixed * b_ref[...]).astype(BF16)
    for k in range(heads):
        work_ref[:, cols(k)] = dot(d_mixed_ref[:, cols(k)], normed_ref[:, cols(k)], NT)
    for k in range(heads):
        weights = weights_ref[:, cols(k)].astype(F32)
        d_weights = work_ref[:, cols(k)]
        inner = jnp.sum(weights * d_weights, axis=-1, keepdims=True)
        d_scores = weights * (d_weights - inner) * (1.0 / HD)
        both_ref[:, cols(k)] = (d_scores + d_scores.T).astype(BF16)
    for k in range(heads):
        work_ref[:, cols(k)] = dot(weights_ref[:, cols(k)].T, d_mixed_ref[:, cols(k)], NN) + dot(
            both_ref[:, cols(k)], normed_ref[:, cols(k)], NN
        )
    for k in range(heads):
        x = x_ref[:, cols(k)].astype(F32)
        grads_ref[0:1, cols(k)] = jnp.sum(work_ref[:, cols(k)] * (x * scale_ref[...]), axis=0, keepdims=True)
    if dx_ref is None:
        return
    products = jnp.zeros((rows, HD), F32)
    for k in range(heads):
        d_pre = work_ref[:, cols(k)] * gain_of(0, k)
        products = products + d_pre * x_ref[:, cols(k)].astype(F32)
    x_scale = scale_ref[...]
    b_ref[...] = x_scale * x_scale * x_scale * spread(mean_of(products, width), rows)
    for k in range(heads):
        x = x_ref[:, cols(k)].astype(F32)
        dy = dy_ref[:, cols(k)].astype(F32)
        d_pre = work_ref[:, cols(k)] * gain_of(0, k)
        dx_ref[:, cols(k)] = (scale_ref[...] * d_pre - x * b_ref[...] + dy).astype(BF16)


def gains_in(ref, relay=None):
    if relay is None:
        return lambda which, k: ref[which : which + 1, cols(k)]
    return lambda which, k: ref[relay, which : which + 1, cols(k)]


def arrive(x, dy, x_ref, dy_ref, gains_hbm, gains_ref, bias_hbm, bias_ref, sems):
    loads = copies(x, x_ref, sems) if x is not None else []
    small = [
        pltpu.make_async_copy(gains_hbm, gains_ref, sems.at[PIECES]),
        pltpu.make_async_copy(bias_hbm, bias_ref, sems.at[PIECES + 1]),
    ]
    start_all(loads)
    start_all(small)
    load_dy = None
    if dy is not None:
        load_dy = pltpu.make_async_copy(dy, dy_ref, sems.at[PIECES + 2])
        load_dy.start()
    wait_all(small)
    return loads, load_dy


def pick_kernel(
    relay_ref, saved_hbm, act_hbm, own_hbm, mirrored_hbm, saved_out, act_out, saved_ref, act_ref, own_ref, mirrored_ref, sems
):
    relay = relay_ref[0]
    rows, width = act_ref.shape
    loads = [
        pltpu.make_async_copy(saved_hbm.at[relay, 1, 0, 0], saved_ref.at[:rows], sems.at[0]),
        pltpu.make_async_copy(act_hbm.at[relay, 0, 0], act_ref, sems.at[1]),
    ]
    small = [
        pltpu.make_async_copy(own_hbm, own_ref, sems.at[4]),
        pltpu.make_async_copy(mirrored_hbm, mirrored_ref, sems.at[5]),
    ]
    stores = [
        pltpu.make_async_copy(saved_ref, saved_out, sems.at[2]),
        pltpu.make_async_copy(act_ref, act_out, sems.at[3]),
    ]
    start_all(small)
    start_all(loads)
    wait_all(small)
    pair = jnp.where(relay == 0, own_ref[...].astype(F32), mirrored_ref[...].astype(F32))
    top = lax.broadcasted_iota(jnp.int32, (TAIL, width), 0) == 0
    saved_ref[rows:] = jnp.where(top, pair[0:1], pair[1:2]).astype(BF16)
    for load, store in zip(loads, stores):
        load.wait()
        store.start()
    wait_all(stores)


def hold_kernel(way_hbm, small_hbm, way_out, out_ref, sems):
    move = pltpu.make_async_copy(small_hbm, out_ref, sems.at[0])
    move.start()
    move.wait()


def look_kernel(far_hbm, first_hbm, out_ref, sems):
    look = pltpu.make_async_copy(first_hbm, out_ref, sems.at[0])
    look.start()
    look.wait()


def backward_down_kernel(
    x_hbm, dy_hbm, own_hbm, bias_hbm, after, dx_ref, grads_ref, own_ref, x_ref, dy_ref, gains_ref, bias_ref, sems, *refs
):
    loads, load_dy = arrive(
        x_hbm.at[0, 0, 0, 0], dy_hbm.at[0, 0, 0], x_ref, dy_ref, own_hbm, own_ref, bias_hbm, bias_ref, sems
    )
    gains_ref[...] = own_ref[...].astype(F32)
    backward_section(x_ref, loads, load_dy, dy_ref, gains_in(gains_ref), bias_ref, dx_ref, grads_ref, refs)


def backward_up_kernel(
    x_hbm, dy_hbm, own_hbm, mirrored_hbm, bias_hbm, after, dx_ref, grads_ref, all_gains,
    own_ref, mirrored_ref, x_ref, dy_ref, gains_ref, bias_ref, sems, *refs
):
    load_own = pltpu.make_async_copy(own_hbm, own_ref, sems.at[PIECES + 3])
    load_own.start()
    loads, load_dy = arrive(
        x_hbm.at[1, 0, 0, 0], dy_hbm.at[1, 0, 0], x_ref, dy_ref, mirrored_hbm, mirrored_ref, bias_hbm, bias_ref, sems
    )
    load_own.wait()
    gains_ref[...] = mirrored_ref[...].astype(F32)
    all_gains[0] = own_ref[...].astype(F32)
    all_gains[1] = gains_ref[...]
    backward_section(x_ref, loads, load_dy, dy_ref, gains_in(gains_ref), bias_ref, dx_ref, grads_ref, refs)


def backward_next_kernel(
    near, choice_ref, x_hbm, gains_hbm, first_hbm, second_hbm, bias_hbm, after, also, grads_ref,
    tail_ref, x_ref, dy_ref, gains_ref, bias_ref, sems, *refs
):
    rows = x_ref.shape[0]
    loads = copies(x_hbm.at[:rows], x_ref, sems)
    load_dy = pltpu.make_async_copy(first_hbm, dy_ref, sems.at[PIECES + 2])
    load_other = pltpu.make_async_copy(second_hbm, dy_ref, sems.at[PIECES + 2])
    start_all(loads)

    @pl.when(choice_ref[0] == 0)
    def _():
        load_dy.start()

    @pl.when(choice_ref[0] == 1)
    def _():
        load_other.start()

    tail = x_hbm.at[rows:] if near else gains_hbm
    arrive(None, None, x_ref, None, tail, tail_ref, bias_hbm, bias_ref, sems)
    gains_ref[...] = tail_ref[...].astype(F32)[:2]
    backward_section(x_ref, loads, load_dy, dy_ref, gains_in(gains_ref), bias_ref, None, grads_ref, refs)


def forward_near_kernel(
    relay_ref, act_hbm, block_hbm, gains_hbm, bias_hbm, early_hbm, out_ref, early_ref,
    tail_ref, tail_gains_ref, once_ref, x_ref, gains_ref, bias_ref, sems, *refs
):
    relay = relay_ref[0]
    load_early = pltpu.make_async_copy(early_hbm, early_ref, sems.at[PIECES + 4])
    load_tail = pltpu.make_async_copy(block_hbm.at[block_hbm.shape[0] - TAIL :], tail_ref, sems.at[PIECES + 3])
    load_early.start()
    load_tail.start()
    loads, _ = arrive(
        act_hbm, None, x_ref, None, gains_hbm.at[relay], gains_ref, bias_hbm, bias_ref, sems
    )
    load_tail.wait()
    tail_gains_ref[...] = tail_ref[...].astype(F32)[:2]
    forward_section(x_ref, loads, gains_in(tail_gains_ref), bias_ref, once_ref, *refs)
    forward_section(once_ref, [], gains_in(gains_ref), bias_ref, out_ref, *refs)
    load_early.wait()


def forward_once_kernel(
    by_way_ref, direct_hbm, passed_hbm, far_gains_hbm, bias_hbm, early_hbm, after, out_ref, early_ref, tail_ref, x_ref,
    gains_ref, bias_ref, sems, *refs
):
    load_early = pltpu.make_async_copy(early_hbm, early_ref, sems.at[PIECES + 3])
    load_early.start()
    direct = copies(direct_hbm, x_ref, sems)
    passed = copies(passed_hbm, x_ref, sems)

    @pl.when(by_way_ref[0] == 1)
    def _():
        start_all(passed)

    @pl.when(by_way_ref[0] == 0)
    def _():
        start_all(direct)

    arrive(None, None, x_ref, None, far_gains_hbm, tail_ref, bias_hbm, bias_ref, sems)
    gains_ref[...] = tail_ref[...].astype(F32)
    forward_section(x_ref, direct, gains_in(gains_ref), bias_ref, out_ref, *refs)
    load_early.wait()


def forward_far_kernel(
    relay_ref, x_hbm, gains_hbm, bias_hbm, near_hbm, early_hbm, out_ref, early_ref, x_ref, gains_ref, bias_ref, sems, *refs
):
    relay = relay_ref[0]
    load_early = pltpu.make_async_copy(early_hbm, early_ref, sems.at[PIECES + 2])
    load_near = pltpu.make_async_copy(near_hbm, out_ref.at[1 - relay, 0, 0], sems.at[PIECES + 3])
    load_early.start()
    load_near.start()
    loads, _ = arrive(x_hbm, None, x_ref, None, gains_hbm.at[relay], gains_ref, bias_hbm, bias_ref, sems)
    forward_section(x_ref, loads, gains_in(gains_ref), bias_ref, out_ref.at[relay, 0, 0], *refs)
    load_near.wait()
    load_early.wait()


SMALL = pl.BlockSpec(memory_space=pltpu.SMEM)
NEAR = pl.BlockSpec(memory_space=pltpu.VMEM)
FAR = pl.BlockSpec(memory_space=pl.ANY)
PLAIN = pl.BlockSpec(memory_space=pltpu.HBM)


def call(kernel, name, operands, out_specs, out_shape, held, rows, width, kind, vmem=PART):
    block = pltpu.VMEM((rows, width), BF16)
    scratch = [block if h is None else h for h in held]
    if kind > 0:
        scratch += [
            pltpu.VMEM((2, width), F32),
            pltpu.VMEM((rows, rows), F32),
            pltpu.SemaphoreType.DMA((PIECES + 5,)),
            block,
            block,
            pltpu.VMEM((rows, width), F32),
            pltpu.VMEM((rows, HD), F32),
        ]
    if kind > 1:
        scratch += [pltpu.VMEM((rows, HD), F32), pltpu.VMEM((rows, HD), F32), block, block, pltpu.VMEM((rows, width), F32)]
    return pl.pallas_call(
        kernel,
        out_shape=out_shape,
        in_specs=[SMALL if x.dtype == jnp.int32 else PLAIN if x.ndim > 4 else FAR for x in operands],
        out_specs=out_specs,
        scratch_shapes=scratch,
        compiler_params=pltpu.CompilerParams(vmem_limit_bytes=vmem),
        cost_estimate=pl.CostEstimate(flops=0, bytes_accessed=COST, transcendentals=0),
        name=name,
    )(*operands)


def shape(*sizes, dtype=BF16):
    return jax.ShapeDtypeStruct(sizes, dtype)


def pick(relay, saved, act, own, mirrored):
    rows, width = act.shape[-2:]
    small = pltpu.VMEM((2, width), BF16)
    return call(
        pick_kernel, "pick", (relay, saved, act, own, mirrored), (FAR, FAR), (shape(rows + TAIL, width), shape(rows, width)),
        [pltpu.VMEM((rows + TAIL, width), BF16), None, small, small, pltpu.SemaphoreType.DMA((6,))], rows, width, 0, FULL,
    )


def hold(way, small):
    return pl.pallas_call(
        hold_kernel,
        out_shape=(shape(*way.shape), shape(*small.shape, dtype=F32)),
        in_specs=[FAR, FAR],
        out_specs=(FAR, NEAR),
        scratch_shapes=[pltpu.SemaphoreType.DMA((1,))],
        input_output_aliases={0: 0},
        compiler_params=pltpu.CompilerParams(vmem_limit_bytes=MEBI),
        cost_estimate=pl.CostEstimate(flops=0, bytes_accessed=COST, transcendentals=0),
        name="hold",
    )(way, small)


def look(far, first):
    rows, width = far.shape
    return call(
        look_kernel, "look", (far, first), NEAR, shape(*first.shape, dtype=F32), [pltpu.SemaphoreType.DMA((1,))],
        rows, width, 0,
    )


def backward_down(x, dy, own, bias, after):
    rows, width = x.shape[-2:]
    return call(
        backward_down_kernel, "backward_down", (x, dy, own, bias, after), (NEAR, NEAR),
        (shape(rows, width), shape(2, width, dtype=F32)), [pltpu.VMEM((2, width), BF16), None, None], rows, width, 2, MOST,
    )


def backward_up(x, dy, own, mirrored, bias, after):
    rows, width = x.shape[-2:]
    small = pltpu.VMEM((2, width), BF16)
    return call(
        backward_up_kernel, "backward_up", (x, dy, own, mirrored, bias, after), (NEAR,) * 3,
        (shape(rows, width), shape(2, width, dtype=F32), shape(2, 2, width, dtype=F32)),
        [small, small, None, None], rows, width, 2, MOST,
    )


def backward_next(near, choice, x, gains, first, second, bias, after, also):
    rows, width = first.shape
    return call(
        functools.partial(backward_next_kernel, near), "backward_next",
        (choice, x, gains, first, second, bias, after, also),
        NEAR, shape(2, width, dtype=F32), [pltpu.VMEM((TAIL if near else 2, width), BF16), None, None], rows, width, 2,
    )


def forward_near(relay, act, tail, gains, bias, early):
    rows, width = act.shape
    return call(
        forward_near_kernel, "forward_near", (relay, act, tail, gains, bias, early), (NEAR, NEAR),
        (shape(rows, width), shape(*early.shape, dtype=F32)),
        [pltpu.VMEM((TAIL, width), BF16), pltpu.VMEM((2, width), F32), None, None], rows, width, 1,
    )


def forward_once(by_way, direct, passed, far_gains, bias, early, after):
    rows, width = direct.shape
    return call(
        forward_once_kernel, "forward_once", (by_way, direct, passed, far_gains, bias, early, after), (NEAR, NEAR),
        (shape(rows, width), shape(*early.shape, dtype=F32)), [pltpu.VMEM((2, width), BF16), None], rows, width, 1,
    )


def forward_far(relay, x, gains, bias, near, early):
    rows, width = x.shape
    return call(
        forward_far_kernel, "forward_far", (relay, x, gains, bias, near, early), (NEAR, NEAR),
        (shape(2, 1, 1, rows, width), shape(*early.shape, dtype=F32)), [None], rows, width, 1,
    )


def summed_along(value, total, axis, stride, size):
    for step in range(1, size):
        pairs = []
        for i in range(lax.axis_size(axis)):
            place = i // stride % size
            pairs.append((i, i + ((place + step) % size - place) * stride))
        total = total + lax.ppermute(value, axis, pairs)
    return total


def routes(count):
    low, high, last = count // 2 - 1, count // 2, count - 1
    near = [(i, i ^ 1) for i in range(count)]
    far = [(i, i + 1) for i in range(1, last, 2) if i != low]
    far = far + [(b, a) for a, b in far]
    straight = [(low, high), (high, low)]
    out = [(low, 0), (high, last)]
    on = [(0, high), (last, low)]
    return near, far, straight, out, on


def body(act_in, grad_in, saved_inputs, first_key, norm_gains):
    rows = act_in.shape[3]
    count = lax.axis_size("section")
    last = count - 1
    near, far, straight, out, on = routes(count)
    mirror = [(i, last - i) for i in range(count)]
    section = lax.axis_index("section")
    odd = section % 2
    ends = (section == count // 2 - 1) | (section == count // 2)
    outer = jnp.stack([1 - odd]).astype(jnp.int32)
    inner = jnp.stack([odd]).astype(jnp.int32)
    by_way = jnp.stack([ends]).astype(jnp.int32)

    own = norm_gains[0]
    mirrored = lax.ppermute(own, "section", mirror)
    query = lax.broadcasted_iota(jnp.int32, (rows, rows), 0)
    key = lax.broadcasted_iota(jnp.int32, (rows, rows), 1)
    visible = (key <= query) & (key >= first_key[0][:, None])
    bias = jnp.where(visible, 0.0, HIDDEN).astype(F32)
    far_sent, act_sent = pick(outer, saved_inputs, act_in, own, own)
    near_sent, near_act = pick(inner, saved_inputs, act_in, own, mirrored)
    far_block = lax.ppermute(far_sent, "section", far + straight)
    half_way = lax.ppermute(act_sent, "section", out)
    far_act = lax.ppermute(act_sent, "section", far)
    near_block = lax.ppermute(near_sent, "section", near)
    near_act = lax.ppermute(near_act, "section", near)
    far_gains = lax.ppermute(jnp.where(odd == 1, own, mirrored), "section", far + straight)

    dx_down, first_down = backward_down(saved_inputs, grad_in, own, bias, own)
    half_way, first_down = hold(half_way, first_down)
    passed_act = lax.ppermute(half_way, "section", on)
    dx_up, first_up, gains = backward_up(saved_inputs, grad_in, own, mirrored, bias, first_down)
    near_out, first_up = forward_near(outer, near_act, near_block, gains, bias, first_up)
    first_up = look(far_block, first_up)
    far_second = backward_next(False, inner, far_block, far_gains, dx_down, dx_up, bias, first_up, first_up)
    near_second = backward_next(True, inner, near_block, gains, dx_up, dx_down, bias, far_second, far_act)
    there = lax.ppermute(first_up, "section", mirror)
    down = jnp.where(odd == 1, near_second, far_second)
    up = jnp.where(odd == 1, far_second, near_second)
    down = lax.ppermute(down, "section", [(i, i - 1) for i in range(1, count)])
    up = lax.ppermute(up, "section", [(i, last - 1 - i) for i in range(last)])
    once, here = forward_once(by_way, far_act, passed_act, far_gains, bias, first_down, near_second)
    total = here + there + down + up
    outputs, same = forward_far(inner, once, gains, bias, near_out, total)
    part = summed_along(total, same, "dp", 1, 4)
    combined = summed_along(part, part, "dp", 4, lax.axis_size("dp") // 4)
    return (outputs, combined[None])


def solution(mesh):
    placed = (
        P(None, "section", "dp", None, None),
        P(None, "section", "dp", None, None),
        P(None, None, "section", "dp", None, None),
        P("dp", None),
        P("section", None, None),
    )
    return jax.shard_map(
        body,
        mesh=mesh,
        in_specs=placed,
        out_specs=(P(None, "section", "dp", None, None), P("section", None, None)),
        check_vma=False,
    )
```

```python
import jax
import jax.numpy as jnp
from jax import lax
from jax.experimental import pallas as pl
from jax.experimental.pallas import tpu as pltpu
from jax.sharding import PartitionSpec as P

HD = 128
EPSILON = 1e-06
LOG2E = 1.4426950408889634
HIDDEN = -1e30
PIECES = 4
COST = 200_000
MEBI = 1024 * 1024
FULL = 60 * MEBI
MOST = 48 * MEBI
PART = 30 * MEBI
TAIL = 16
F32 = jnp.float32
BF16 = jnp.bfloat16

NT = (((1,), (1,)), ((), ()))
NN = (((1,), (0,)), ((), ()))


def dot(a, b, dims):
    return lax.dot_general(a, b, dims, preferred_element_type=F32)


def cols(k):
    return slice(k * HD, (k + 1) * HD)


def mean_of(total, width):
    return jnp.sum(total, axis=-1, keepdims=True) * (1.0 / width)


def spread(column, rows):
    return jnp.broadcast_to(column, (rows, HD))


def pieces(heads):
    step = -(-heads // PIECES)
    return [(low, min(low + step, heads)) for low in range(0, heads, step)]


def copies(source, target, sems, first=0):
    heads = target.shape[1] // HD
    parts = [slice(low * HD, high * HD) for low, high in pieces(heads)]
    return [
        pltpu.make_async_copy(source.at[:, part], target.at[:, part], sems.at[first + i]) for i, part in enumerate(parts)
    ]


def start_all(moves):
    for move in moves:
        move.start()


def wait_all(moves):
    for move in moves:
        move.wait()


def attention(x_ref, waits, gain_of, bias_ref, normed_ref, scores_ref, weights_ref, scale_ref):
    rows, width = x_ref.shape
    heads = width // HD
    acc = jnp.zeros((rows, HD), F32)
    for i, (low, high) in enumerate(pieces(heads)):
        if waits:
            waits[i].wait()
        for k in range(low, high):
            x = x_ref[:, cols(k)].astype(F32)
            acc = acc + x * x
    scale_ref[...] = spread(lax.rsqrt(mean_of(acc, width) + EPSILON), rows)
    for k in range(heads):
        x = x_ref[:, cols(k)].astype(F32)
        normed_ref[:, cols(k)] = (x * scale_ref[...] * gain_of(0, k)).astype(BF16)
    for k in range(heads):
        normed = normed_ref[:, cols(k)]
        scores_ref[:, cols(k)] = dot(normed, normed, NT)
    for k in range(heads):
        raised = jnp.exp2(scores_ref[:, cols(k)] * (LOG2E / HD) + bias_ref[...])
        total = jnp.sum(raised, axis=-1, keepdims=True)
        weights_ref[:, cols(k)] = (raised * (1.0 / total)).astype(BF16)
    for k in range(heads):
        scores_ref[:, cols(k)] = dot(weights_ref[:, cols(k)], normed_ref[:, cols(k)], NN)


def forward_section(x_ref, waits, gain_of, bias_ref, out_ref, normed_ref, weights_ref, mixed_ref, scale_ref):
    rows, width = x_ref.shape
    heads = width // HD
    attention(x_ref, waits, gain_of, bias_ref, normed_ref, mixed_ref, weights_ref, scale_ref)
    acc = jnp.zeros((rows, HD), F32)
    for k in range(heads):
        mixed = mixed_ref[:, cols(k)]
        acc = acc + mixed * mixed
    scale_ref[...] = spread(lax.rsqrt(mean_of(acc, width) + EPSILON), rows)
    for k in range(heads):
        x = x_ref[:, cols(k)].astype(F32)
        out_ref[:, cols(k)] = (x + mixed_ref[:, cols(k)] * scale_ref[...] * gain_of(1, k)).astype(BF16)


def backward_section(x_ref, waits, wait_dy, dy_ref, gain_of, bias_ref, dx_ref, grads_ref, refs):
    normed_ref, weights_ref, mixed_ref, scale_ref, m_ref, b_ref, d_mixed_ref, both_ref, work_ref = refs
    rows, width = x_ref.shape
    heads = width // HD
    attention(x_ref, waits, gain_of, bias_ref, normed_ref, mixed_ref, weights_ref, scale_ref)
    wait_dy.wait()
    squares = products = jnp.zeros((rows, HD), F32)
    for k in range(heads):
        mixed = mixed_ref[:, cols(k)]
        post_grad = dy_ref[:, cols(k)].astype(F32) * gain_of(1, k)
        squares = squares + mixed * mixed
        products = products + post_grad * mixed
    m_scale = lax.rsqrt(mean_of(squares, width) + EPSILON)
    m_ref[...] = spread(m_scale, rows)
    b_ref[...] = spread(m_scale * m_scale * m_scale * mean_of(products, width), rows)
    for k in range(heads):
        mixed = mixed_ref[:, cols(k)]
        scaled = dy_ref[:, cols(k)].astype(F32) * m_ref[...]
        grads_ref[1:2, cols(k)] = jnp.sum(scaled * mixed, axis=0, keepdims=True)
        d_mixed_ref[:, cols(k)] = (scaled * gain_of(1, k) - mixed * b_ref[...]).astype(BF16)
    for k in range(heads):
        work_ref[:, cols(k)] = dot(d_mixed_ref[:, cols(k)], normed_ref[:, cols(k)], NT)
    for k in range(heads):
        weights = weights_ref[:, cols(k)].astype(F32)
        d_weights = work_ref[:, cols(k)]
        inner = jnp.sum(weights * d_weights, axis=-1, keepdims=True)
        d_scores = weights * (d_weights - inner) * (1.0 / HD)
        both_ref[:, cols(k)] = (d_scores + d_scores.T).astype(BF16)
    for k in range(heads):
        work_ref[:, cols(k)] = dot(weights_ref[:, cols(k)].T, d_mixed_ref[:, cols(k)], NN) + dot(
            both_ref[:, cols(k)], normed_ref[:, cols(k)], NN
        )
    for k in range(heads):
        x = x_ref[:, cols(k)].astype(F32)
        grads_ref[0:1, cols(k)] = jnp.sum(work_ref[:, cols(k)] * (x * scale_ref[...]), axis=0, keepdims=True)
    if dx_ref is None:
        return
    products = jnp.zeros((rows, HD), F32)
    for k in range(heads):
        d_pre = work_ref[:, cols(k)] * gain_of(0, k)
        products = products + d_pre * x_ref[:, cols(k)].astype(F32)
    x_scale = scale_ref[...]
    b_ref[...] = x_scale * x_scale * x_scale * spread(mean_of(products, width), rows)
    for k in range(heads):
        x = x_ref[:, cols(k)].astype(F32)
        dy = dy_ref[:, cols(k)].astype(F32)
        d_pre = work_ref[:, cols(k)] * gain_of(0, k)
        dx_ref[:, cols(k)] = (scale_ref[...] * d_pre - x * b_ref[...] + dy).astype(BF16)


def gains_in(ref, relay=None):
    if relay is None:
        return lambda which, k: ref[which : which + 1, cols(k)]
    return lambda which, k: ref[relay, which : which + 1, cols(k)]


def arrive(x, dy, x_ref, dy_ref, gains_hbm, gains_ref, bias_hbm, bias_ref, sems):
    loads = copies(x, x_ref, sems) if x is not None else []
    small = [
        pltpu.make_async_copy(gains_hbm, gains_ref, sems.at[PIECES]),
        pltpu.make_async_copy(bias_hbm, bias_ref, sems.at[PIECES + 1]),
    ]
    start_all(loads)
    start_all(small)
    load_dy = None
    if dy is not None:
        load_dy = pltpu.make_async_copy(dy, dy_ref, sems.at[PIECES + 2])
        load_dy.start()
    wait_all(small)
    return loads, load_dy


def pick_kernel(
    relay_ref, saved_hbm, act_hbm, own_hbm, mirrored_hbm, far_out, far_act, near_out, near_act,
    far_ref, far_act_ref, near_ref, near_act_ref, own_ref, mirrored_ref, sems
):
    outer = relay_ref[0]
    inner = 1 - outer
    rows, width = far_act_ref.shape
    loads = [
        pltpu.make_async_copy(saved_hbm.at[outer, 1, 0, 0], far_ref.at[:rows], sems.at[0]),
        pltpu.make_async_copy(act_hbm.at[outer, 0, 0], far_act_ref, sems.at[1]),
        pltpu.make_async_copy(saved_hbm.at[inner, 1, 0, 0], near_ref.at[:rows], sems.at[2]),
        pltpu.make_async_copy(act_hbm.at[inner, 0, 0], near_act_ref, sems.at[3]),
    ]
    small = [
        pltpu.make_async_copy(own_hbm, own_ref, sems.at[4]),
        pltpu.make_async_copy(mirrored_hbm, mirrored_ref, sems.at[5]),
    ]
    stores = [
        pltpu.make_async_copy(far_ref, far_out, sems.at[6]),
        pltpu.make_async_copy(far_act_ref, far_act, sems.at[7]),
        pltpu.make_async_copy(near_ref, near_out, sems.at[8]),
        pltpu.make_async_copy(near_act_ref, near_act, sems.at[9]),
    ]
    start_all(small)
    start_all(loads)
    wait_all(small)
    own = own_ref[...].astype(F32)
    mirrored = mirrored_ref[...].astype(F32)
    top = lax.broadcasted_iota(jnp.int32, (TAIL, width), 0) == 0
    for ref, relay in ((far_ref, outer), (near_ref, inner)):
        pair = jnp.where(relay == 0, own, mirrored)
        ref[rows:] = jnp.where(top, pair[0:1], pair[1:2]).astype(BF16)
    for load, store in zip(loads, stores):
        load.wait()
        store.start()
    wait_all(stores)


def hold_kernel(way_hbm, small_hbm, way_out, out_ref, sems):
    move = pltpu.make_async_copy(small_hbm, out_ref, sems.at[0])
    move.start()
    move.wait()


def look_kernel(far_hbm, first_hbm, out_ref, sems):
    look = pltpu.make_async_copy(first_hbm, out_ref, sems.at[0])
    look.start()
    look.wait()


def backward_down_kernel(
    x_hbm, dy_hbm, own_hbm, bias_hbm, after, dx_ref, grads_ref, own_ref, x_ref, dy_ref, gains_ref, bias_ref, sems, *refs
):
    loads, load_dy = arrive(
        x_hbm.at[0, 0, 0, 0], dy_hbm.at[0, 0, 0], x_ref, dy_ref, own_hbm, own_ref, bias_hbm, bias_ref, sems
    )
    gains_ref[...] = own_ref[...].astype(F32)
    backward_section(x_ref, loads, load_dy, dy_ref, gains_in(gains_ref), bias_ref, dx_ref, grads_ref, refs)


def backward_up_kernel(
    x_hbm, dy_hbm, own_hbm, mirrored_hbm, bias_hbm, after, dx_ref, grads_ref, all_gains,
    own_ref, mirrored_ref, x_ref, dy_ref, gains_ref, bias_ref, sems, *refs
):
    load_own = pltpu.make_async_copy(own_hbm, own_ref, sems.at[PIECES + 3])
    load_own.start()
    loads, load_dy = arrive(
        x_hbm.at[1, 0, 0, 0], dy_hbm.at[1, 0, 0], x_ref, dy_ref, mirrored_hbm, mirrored_ref, bias_hbm, bias_ref, sems
    )
    load_own.wait()
    gains_ref[...] = mirrored_ref[...].astype(F32)
    all_gains[0] = own_ref[...].astype(F32)
    all_gains[1] = gains_ref[...]
    backward_section(x_ref, loads, load_dy, dy_ref, gains_in(gains_ref), bias_ref, dx_ref, grads_ref, refs)


def backward_next_kernel(
    choice_ref, x_hbm, first_hbm, second_hbm, bias_hbm, after, also, grads_ref,
    tail_ref, x_ref, dy_ref, gains_ref, bias_ref, sems, *refs
):
    rows = x_ref.shape[0]
    loads = copies(x_hbm.at[:rows], x_ref, sems)
    load_dy = pltpu.make_async_copy(first_hbm, dy_ref, sems.at[PIECES + 2])
    load_other = pltpu.make_async_copy(second_hbm, dy_ref, sems.at[PIECES + 2])
    start_all(loads)

    @pl.when(choice_ref[0] == 0)
    def _():
        load_dy.start()

    @pl.when(choice_ref[0] == 1)
    def _():
        load_other.start()

    arrive(None, None, x_ref, None, x_hbm.at[rows:], tail_ref, bias_hbm, bias_ref, sems)
    gains_ref[...] = tail_ref[...].astype(F32)[:2]
    backward_section(x_ref, loads, load_dy, dy_ref, gains_in(gains_ref), bias_ref, None, grads_ref, refs)


def forward_near_kernel(
    relay_ref, act_hbm, block_hbm, gains_hbm, bias_hbm, early_hbm, out_ref, early_ref,
    tail_ref, tail_gains_ref, once_ref, x_ref, gains_ref, bias_ref, sems, *refs
):
    relay = relay_ref[0]
    load_early = pltpu.make_async_copy(early_hbm, early_ref, sems.at[PIECES + 4])
    load_tail = pltpu.make_async_copy(block_hbm.at[block_hbm.shape[0] - TAIL :], tail_ref, sems.at[PIECES + 3])
    load_early.start()
    load_tail.start()
    loads, _ = arrive(
        act_hbm, None, x_ref, None, gains_hbm.at[relay], gains_ref, bias_hbm, bias_ref, sems
    )
    load_tail.wait()
    tail_gains_ref[...] = tail_ref[...].astype(F32)[:2]
    forward_section(x_ref, loads, gains_in(tail_gains_ref), bias_ref, once_ref, *refs)
    forward_section(once_ref, [], gains_in(gains_ref), bias_ref, out_ref, *refs)
    load_early.wait()


def forward_once_kernel(
    by_way_ref, direct_hbm, passed_hbm, far_hbm, bias_hbm, early_hbm, after, out_ref, early_ref, tail_ref, x_ref,
    gains_ref, bias_ref, sems, *refs
):
    load_early = pltpu.make_async_copy(early_hbm, early_ref, sems.at[PIECES + 3])
    load_early.start()
    direct = copies(direct_hbm, x_ref, sems)
    passed = copies(passed_hbm, x_ref, sems)

    @pl.when(by_way_ref[0] == 1)
    def _():
        start_all(passed)

    @pl.when(by_way_ref[0] == 0)
    def _():
        start_all(direct)

    tail = far_hbm.at[far_hbm.shape[0] - TAIL :]
    arrive(None, None, x_ref, None, tail, tail_ref, bias_hbm, bias_ref, sems)
    gains_ref[...] = tail_ref[...].astype(F32)[:2]
    forward_section(x_ref, direct, gains_in(gains_ref), bias_ref, out_ref, *refs)
    load_early.wait()


def forward_far_kernel(
    relay_ref, x_hbm, gains_hbm, bias_hbm, near_hbm, early_hbm, out_ref, early_ref, x_ref, gains_ref, bias_ref, sems, *refs
):
    relay = relay_ref[0]
    load_early = pltpu.make_async_copy(early_hbm, early_ref, sems.at[PIECES + 2])
    load_near = pltpu.make_async_copy(near_hbm, out_ref.at[1 - relay, 0, 0], sems.at[PIECES + 3])
    load_early.start()
    load_near.start()
    loads, _ = arrive(x_hbm, None, x_ref, None, gains_hbm.at[relay], gains_ref, bias_hbm, bias_ref, sems)
    forward_section(x_ref, loads, gains_in(gains_ref), bias_ref, out_ref.at[relay, 0, 0], *refs)
    load_near.wait()
    load_early.wait()


SMALL = pl.BlockSpec(memory_space=pltpu.SMEM)
NEAR = pl.BlockSpec(memory_space=pltpu.VMEM)
FAR = pl.BlockSpec(memory_space=pl.ANY)
PLAIN = pl.BlockSpec(memory_space=pltpu.HBM)


def call(kernel, name, operands, out_specs, out_shape, held, rows, width, kind, vmem=PART):
    block = pltpu.VMEM((rows, width), BF16)
    scratch = [block if h is None else h for h in held]
    if kind > 0:
        scratch += [
            pltpu.VMEM((2, width), F32),
            pltpu.VMEM((rows, rows), F32),
            pltpu.SemaphoreType.DMA((PIECES + 5,)),
            block,
            block,
            pltpu.VMEM((rows, width), F32),
            pltpu.VMEM((rows, HD), F32),
        ]
    if kind > 1:
        scratch += [pltpu.VMEM((rows, HD), F32), pltpu.VMEM((rows, HD), F32), block, block, pltpu.VMEM((rows, width), F32)]
    return pl.pallas_call(
        kernel,
        out_shape=out_shape,
        in_specs=[SMALL if x.dtype == jnp.int32 else PLAIN if x.ndim > 4 else FAR for x in operands],
        out_specs=out_specs,
        scratch_shapes=scratch,
        compiler_params=pltpu.CompilerParams(vmem_limit_bytes=vmem),
        cost_estimate=pl.CostEstimate(flops=0, bytes_accessed=COST, transcendentals=0),
        name=name,
    )(*operands)


def shape(*sizes, dtype=BF16):
    return jax.ShapeDtypeStruct(sizes, dtype)


def pick(relay, saved, act, own, mirrored):
    rows, width = act.shape[-2:]
    small = pltpu.VMEM((2, width), BF16)
    long = pltpu.VMEM((rows + TAIL, width), BF16)
    return call(
        pick_kernel, "pick", (relay, saved, act, own, mirrored), (FAR,) * 4,
        (shape(rows + TAIL, width), shape(rows, width)) * 2,
        [long, None, long, None, small, small, pltpu.SemaphoreType.DMA((10,))], rows, width, 0, FULL,
    )


def hold(way, small):
    return pl.pallas_call(
        hold_kernel,
        out_shape=(shape(*way.shape), shape(*small.shape, dtype=F32)),
        in_specs=[FAR, FAR],
        out_specs=(FAR, NEAR),
        scratch_shapes=[pltpu.SemaphoreType.DMA((1,))],
        input_output_aliases={0: 0},
        compiler_params=pltpu.CompilerParams(vmem_limit_bytes=MEBI),
        cost_estimate=pl.CostEstimate(flops=0, bytes_accessed=COST, transcendentals=0),
        name="hold",
    )(way, small)


def look(far, first):
    rows, width = far.shape
    return call(
        look_kernel, "look", (far, first), NEAR, shape(*first.shape, dtype=F32), [pltpu.SemaphoreType.DMA((1,))],
        rows, width, 0,
    )


def backward_down(x, dy, own, bias, after):
    rows, width = x.shape[-2:]
    return call(
        backward_down_kernel, "backward_down", (x, dy, own, bias, after), (NEAR, NEAR),
        (shape(rows, width), shape(2, width, dtype=F32)), [pltpu.VMEM((2, width), BF16), None, None], rows, width, 2, MOST,
    )


def backward_up(x, dy, own, mirrored, bias, after):
    rows, width = x.shape[-2:]
    small = pltpu.VMEM((2, width), BF16)
    return call(
        backward_up_kernel, "backward_up", (x, dy, own, mirrored, bias, after), (NEAR,) * 3,
        (shape(rows, width), shape(2, width, dtype=F32), shape(2, 2, width, dtype=F32)),
        [small, small, None, None], rows, width, 2, MOST,
    )


def backward_next(choice, x, first, second, bias, after, also):
    rows, width = first.shape
    return call(
        backward_next_kernel, "backward_next", (choice, x, first, second, bias, after, also),
        NEAR, shape(2, width, dtype=F32), [pltpu.VMEM((TAIL, width), BF16), None, None], rows, width, 2,
    )


def forward_near(relay, act, tail, gains, bias, early):
    rows, width = act.shape
    return call(
        forward_near_kernel, "forward_near", (relay, act, tail, gains, bias, early), (NEAR, NEAR),
        (shape(rows, width), shape(*early.shape, dtype=F32)),
        [pltpu.VMEM((TAIL, width), BF16), pltpu.VMEM((2, width), F32), None, None], rows, width, 1,
    )


def forward_once(by_way, direct, passed, far, bias, early, after):
    rows, width = direct.shape
    return call(
        forward_once_kernel, "forward_once", (by_way, direct, passed, far, bias, early, after), (NEAR, NEAR),
        (shape(rows, width), shape(*early.shape, dtype=F32)), [pltpu.VMEM((TAIL, width), BF16), None], rows, width, 1,
    )


def forward_far(relay, x, gains, bias, near, early):
    rows, width = x.shape
    return call(
        forward_far_kernel, "forward_far", (relay, x, gains, bias, near, early), (NEAR, NEAR),
        (shape(2, 1, 1, rows, width), shape(*early.shape, dtype=F32)), [None], rows, width, 1,
    )


def summed_along(value, total, axis, stride, size):
    for step in range(1, size):
        pairs = []
        for i in range(lax.axis_size(axis)):
            place = i // stride % size
            pairs.append((i, i + ((place + step) % size - place) * stride))
        total = total + lax.ppermute(value, axis, pairs)
    return total


def routes(count):
    low, high, last = count // 2 - 1, count // 2, count - 1
    near = [(i, i ^ 1) for i in range(count)]
    far = [(i, i + 1) for i in range(1, last, 2) if i != low]
    far = far + [(b, a) for a, b in far]
    straight = [(low, high), (high, low)]
    out = [(low, 0), (high, last)]
    on = [(0, high), (last, low)]
    return near, far, straight, out, on


def body(act_in, grad_in, saved_inputs, first_key, norm_gains):
    rows = act_in.shape[3]
    count = lax.axis_size("section")
    last = count - 1
    near, far, straight, out, on = routes(count)
    mirror = [(i, last - i) for i in range(count)]
    section = lax.axis_index("section")
    odd = section % 2
    ends = (section == count // 2 - 1) | (section == count // 2)
    outer = jnp.stack([1 - odd]).astype(jnp.int32)
    inner = jnp.stack([odd]).astype(jnp.int32)
    by_way = jnp.stack([ends]).astype(jnp.int32)

    own = norm_gains[0]
    mirrored = lax.ppermute(own, "section", mirror)
    query = lax.broadcasted_iota(jnp.int32, (rows, rows), 0)
    key = lax.broadcasted_iota(jnp.int32, (rows, rows), 1)
    visible = (key <= query) & (key >= first_key[0][:, None])
    bias = jnp.where(visible, 0.0, HIDDEN).astype(F32)
    far_sent, act_sent, near_sent, near_act = pick(outer, saved_inputs, act_in, own, mirrored)
    far_block = lax.ppermute(far_sent, "section", far + straight)
    half_way = lax.ppermute(act_sent, "section", out)
    far_act = lax.ppermute(act_sent, "section", far)
    near_block = lax.ppermute(near_sent, "section", near)
    near_act = lax.ppermute(near_act, "section", near)

    dx_down, first_down = backward_down(saved_inputs, grad_in, own, bias, own)
    half_way, first_down = hold(half_way, first_down)
    passed_act = lax.ppermute(half_way, "section", on)
    dx_up, first_up, gains = backward_up(saved_inputs, grad_in, own, mirrored, bias, first_down)
    near_out, first_up = forward_near(outer, near_act, near_block, gains, bias, first_up)
    first_up = look(far_block, first_up)
    far_second = backward_next(inner, far_block, dx_down, dx_up, bias, first_up, first_up)
    near_second = backward_next(inner, near_block, dx_up, dx_down, bias, far_second, far_act)
    there = lax.ppermute(first_up, "section", mirror)
    down = jnp.where(odd == 1, near_second, far_second)
    up = jnp.where(odd == 1, far_second, near_second)
    down = lax.ppermute(down, "section", [(i, i - 1) for i in range(1, count)])
    up = lax.ppermute(up, "section", [(i, last - 1 - i) for i in range(last)])
    once, here = forward_once(by_way, far_act, passed_act, far_block, bias, first_down, near_second)
    total = here + there + down + up
    outputs, same = forward_far(inner, once, gains, bias, near_out, total)
    part = summed_along(total, same, "dp", 1, 4)
    combined = summed_along(part, part, "dp", 4, lax.axis_size("dp") // 4)
    return (outputs, combined[None])


def solution(mesh):
    placed = (
        P(None, "section", "dp", None, None),
        P(None, "section", "dp", None, None),
        P(None, None, "section", "dp", None, None),
        P("dp", None),
        P("section", None, None),
    )
    return jax.shard_map(
        body,
        mesh=mesh,
        in_specs=placed,
        out_specs=(P(None, "section", "dp", None, None), P("section", None, None)),
        check_vma=False,
    )
```

```python
import jax
import jax.numpy as jnp
from jax import lax
from jax.experimental import pallas as pl
from jax.experimental.pallas import tpu as pltpu
from jax.sharding import PartitionSpec as P

HD = 128
EPSILON = 1e-06
LOG2E = 1.4426950408889634
HIDDEN = -1e30
PIECES = 4
COST = 200_000
MEBI = 1024 * 1024
FULL = 60 * MEBI
MOST = 52 * MEBI
PART = 30 * MEBI
TAIL = 16
F32 = jnp.float32
BF16 = jnp.bfloat16

NT = (((1,), (1,)), ((), ()))
NN = (((1,), (0,)), ((), ()))


def dot(a, b, dims):
    return lax.dot_general(a, b, dims, preferred_element_type=F32)


def cols(k):
    return slice(k * HD, (k + 1) * HD)


def mean_of(total, width):
    return jnp.sum(total, axis=-1, keepdims=True) * (1.0 / width)


def spread(column, rows):
    return jnp.broadcast_to(column, (rows, HD))


def pieces(heads):
    step = -(-heads // PIECES)
    return [(low, min(low + step, heads)) for low in range(0, heads, step)]


def copies(source, target, sems, first=0):
    heads = target.shape[1] // HD
    parts = [slice(low * HD, high * HD) for low, high in pieces(heads)]
    return [
        pltpu.make_async_copy(source.at[:, part], target.at[:, part], sems.at[first + i]) for i, part in enumerate(parts)
    ]


def start_all(moves):
    for move in moves:
        move.start()


def wait_all(moves):
    for move in moves:
        move.wait()


def attention(x_ref, waits, gain_of, bias_ref, normed_ref, scores_ref, weights_ref, scale_ref):
    rows, width = x_ref.shape
    heads = width // HD
    acc = jnp.zeros((rows, HD), F32)
    for i, (low, high) in enumerate(pieces(heads)):
        if waits:
            waits[i].wait()
        for k in range(low, high):
            x = x_ref[:, cols(k)].astype(F32)
            acc = acc + x * x
    scale_ref[...] = spread(lax.rsqrt(mean_of(acc, width) + EPSILON), rows)
    for k in range(heads):
        x = x_ref[:, cols(k)].astype(F32)
        normed_ref[:, cols(k)] = (x * scale_ref[...] * gain_of(0, k)).astype(BF16)
    for k in range(heads):
        normed = normed_ref[:, cols(k)]
        scores_ref[:, cols(k)] = dot(normed, normed, NT)
    for k in range(heads):
        raised = jnp.exp2(scores_ref[:, cols(k)] * (LOG2E / HD) + bias_ref[...])
        total = jnp.sum(raised, axis=-1, keepdims=True)
        weights_ref[:, cols(k)] = (raised * (1.0 / total)).astype(BF16)
    for k in range(heads):
        scores_ref[:, cols(k)] = dot(weights_ref[:, cols(k)], normed_ref[:, cols(k)], NN)


def forward_section(x_ref, waits, gain_of, bias_ref, out_ref, normed_ref, weights_ref, mixed_ref, scale_ref):
    rows, width = x_ref.shape
    heads = width // HD
    attention(x_ref, waits, gain_of, bias_ref, normed_ref, mixed_ref, weights_ref, scale_ref)
    acc = jnp.zeros((rows, HD), F32)
    for k in range(heads):
        mixed = mixed_ref[:, cols(k)]
        acc = acc + mixed * mixed
    scale_ref[...] = spread(lax.rsqrt(mean_of(acc, width) + EPSILON), rows)
    for k in range(heads):
        x = x_ref[:, cols(k)].astype(F32)
        out_ref[:, cols(k)] = (x + mixed_ref[:, cols(k)] * scale_ref[...] * gain_of(1, k)).astype(BF16)


def backward_section(x_ref, waits, wait_dy, dy_ref, gain_of, bias_ref, dx_ref, grads_ref, refs):
    normed_ref, weights_ref, mixed_ref, scale_ref, m_ref, b_ref, d_mixed_ref, both_ref, work_ref = refs
    rows, width = x_ref.shape
    heads = width // HD
    attention(x_ref, waits, gain_of, bias_ref, normed_ref, mixed_ref, weights_ref, scale_ref)
    wait_dy.wait()
    squares = products = jnp.zeros((rows, HD), F32)
    for k in range(heads):
        mixed = mixed_ref[:, cols(k)]
        post_grad = dy_ref[:, cols(k)].astype(F32) * gain_of(1, k)
        squares = squares + mixed * mixed
        products = products + post_grad * mixed
    m_scale = lax.rsqrt(mean_of(squares, width) + EPSILON)
    m_ref[...] = spread(m_scale, rows)
    b_ref[...] = spread(m_scale * m_scale * m_scale * mean_of(products, width), rows)
    for k in range(heads):
        mixed = mixed_ref[:, cols(k)]
        scaled = dy_ref[:, cols(k)].astype(F32) * m_ref[...]
        grads_ref[1:2, cols(k)] = jnp.sum(scaled * mixed, axis=0, keepdims=True)
        d_mixed_ref[:, cols(k)] = (scaled * gain_of(1, k) - mixed * b_ref[...]).astype(BF16)
    for k in range(heads):
        work_ref[:, cols(k)] = dot(d_mixed_ref[:, cols(k)], normed_ref[:, cols(k)], NT)
    for k in range(heads):
        weights = weights_ref[:, cols(k)].astype(F32)
        d_weights = work_ref[:, cols(k)]
        inner = jnp.sum(weights * d_weights, axis=-1, keepdims=True)
        d_scores = weights * (d_weights - inner) * (1.0 / HD)
        both_ref[:, cols(k)] = (d_scores + d_scores.T).astype(BF16)
    for k in range(heads):
        work_ref[:, cols(k)] = dot(weights_ref[:, cols(k)].T, d_mixed_ref[:, cols(k)], NN) + dot(
            both_ref[:, cols(k)], normed_ref[:, cols(k)], NN
        )
    for k in range(heads):
        x = x_ref[:, cols(k)].astype(F32)
        grads_ref[0:1, cols(k)] = jnp.sum(work_ref[:, cols(k)] * (x * scale_ref[...]), axis=0, keepdims=True)
    if dx_ref is None:
        return
    products = jnp.zeros((rows, HD), F32)
    for k in range(heads):
        d_pre = work_ref[:, cols(k)] * gain_of(0, k)
        products = products + d_pre * x_ref[:, cols(k)].astype(F32)
    x_scale = scale_ref[...]
    b_ref[...] = x_scale * x_scale * x_scale * spread(mean_of(products, width), rows)
    for k in range(heads):
        x = x_ref[:, cols(k)].astype(F32)
        dy = dy_ref[:, cols(k)].astype(F32)
        d_pre = work_ref[:, cols(k)] * gain_of(0, k)
        dx_ref[:, cols(k)] = (scale_ref[...] * d_pre - x * b_ref[...] + dy).astype(BF16)


def gains_in(ref, relay=None):
    if relay is None:
        return lambda which, k: ref[which : which + 1, cols(k)]
    return lambda which, k: ref[relay, which : which + 1, cols(k)]


def arrive(x, dy, x_ref, dy_ref, gains_hbm, gains_ref, bias_hbm, bias_ref, sems):
    loads = copies(x, x_ref, sems) if x is not None else []
    small = [
        pltpu.make_async_copy(gains_hbm, gains_ref, sems.at[PIECES]),
        pltpu.make_async_copy(bias_hbm, bias_ref, sems.at[PIECES + 1]),
    ]
    start_all(loads)
    start_all(small)
    load_dy = None
    if dy is not None:
        load_dy = pltpu.make_async_copy(dy, dy_ref, sems.at[PIECES + 2])
        load_dy.start()
    wait_all(small)
    return loads, load_dy


def pick_kernel(
    relay_ref, saved_hbm, act_hbm, own_hbm, mirrored_hbm, far_out, far_act, near_out, near_act,
    far_ref, far_act_ref, near_ref, near_act_ref, own_ref, mirrored_ref, sems
):
    outer = relay_ref[0]
    inner = 1 - outer
    rows, width = far_act_ref.shape
    loads = [
        pltpu.make_async_copy(saved_hbm.at[outer, 1, 0, 0], far_ref.at[:rows], sems.at[0]),
        pltpu.make_async_copy(act_hbm.at[outer, 0, 0], far_act_ref, sems.at[1]),
        pltpu.make_async_copy(saved_hbm.at[inner, 1, 0, 0], near_ref.at[:rows], sems.at[2]),
        pltpu.make_async_copy(act_hbm.at[inner, 0, 0], near_act_ref, sems.at[3]),
    ]
    small = [
        pltpu.make_async_copy(own_hbm, own_ref, sems.at[4]),
        pltpu.make_async_copy(mirrored_hbm, mirrored_ref, sems.at[5]),
    ]
    stores = [
        pltpu.make_async_copy(far_ref, far_out, sems.at[6]),
        pltpu.make_async_copy(far_act_ref, far_act, sems.at[7]),
        pltpu.make_async_copy(near_ref, near_out, sems.at[8]),
        pltpu.make_async_copy(near_act_ref, near_act, sems.at[9]),
    ]
    start_all(small)
    start_all(loads)
    wait_all(small)
    own = own_ref[...].astype(F32)
    mirrored = mirrored_ref[...].astype(F32)
    top = lax.broadcasted_iota(jnp.int32, (TAIL, width), 0) == 0
    for ref, relay in ((far_ref, outer), (near_ref, inner)):
        pair = jnp.where(relay == 0, own, mirrored)
        ref[rows:] = jnp.where(top, pair[0:1], pair[1:2]).astype(BF16)
    for load, store in zip(loads, stores):
        load.wait()
        store.start()
    wait_all(stores)


def hold_kernel(way_hbm, small_hbm, way_out, out_ref, sems):
    move = pltpu.make_async_copy(small_hbm, out_ref, sems.at[0])
    move.start()
    move.wait()


def look_kernel(far_hbm, first_hbm, out_ref, sems):
    look = pltpu.make_async_copy(first_hbm, out_ref, sems.at[0])
    look.start()
    look.wait()


def backward_first_kernel(
    x_hbm, dy_hbm, own_hbm, mirrored_hbm, bias_hbm, dx_down, dx_up, down_ref, up_ref, all_gains,
    own_ref, mirrored_ref, x_up, dy_up, up_gains_ref, up_sems, x_ref, dy_ref, gains_ref, bias_ref, sems, *refs
):
    loads, load_dy = arrive(
        x_hbm.at[0, 0, 0, 0], dy_hbm.at[0, 0, 0], x_ref, dy_ref, own_hbm, own_ref, bias_hbm, bias_ref, sems
    )
    gains_ref[...] = own_ref[...].astype(F32)
    more = [
        pltpu.make_async_copy(x_hbm.at[1, 0, 0, 0], x_up, up_sems.at[0]),
        pltpu.make_async_copy(dy_hbm.at[1, 0, 0], dy_up, up_sems.at[1]),
        pltpu.make_async_copy(mirrored_hbm, mirrored_ref, up_sems.at[2]),
    ]
    start_all(more)
    backward_section(x_ref, loads, load_dy, dy_ref, gains_in(gains_ref), bias_ref, dx_down, down_ref, refs)
    wait_all(more[::2])
    up_gains_ref[...] = mirrored_ref[...].astype(F32)
    all_gains[0] = gains_ref[...]
    all_gains[1] = up_gains_ref[...]
    backward_section(x_up, [], more[1], dy_up, gains_in(up_gains_ref), bias_ref, dx_up, up_ref, refs)


def backward_next_kernel(
    choice_ref, x_hbm, first_hbm, second_hbm, bias_hbm, after, also, grads_ref,
    tail_ref, x_ref, dy_ref, gains_ref, bias_ref, sems, *refs
):
    rows = x_ref.shape[0]
    loads = copies(x_hbm.at[:rows], x_ref, sems)
    load_dy = pltpu.make_async_copy(first_hbm, dy_ref, sems.at[PIECES + 2])
    load_other = pltpu.make_async_copy(second_hbm, dy_ref, sems.at[PIECES + 2])
    start_all(loads)

    @pl.when(choice_ref[0] == 0)
    def _():
        load_dy.start()

    @pl.when(choice_ref[0] == 1)
    def _():
        load_other.start()

    arrive(None, None, x_ref, None, x_hbm.at[rows:], tail_ref, bias_hbm, bias_ref, sems)
    gains_ref[...] = tail_ref[...].astype(F32)[:2]
    backward_section(x_ref, loads, load_dy, dy_ref, gains_in(gains_ref), bias_ref, None, grads_ref, refs)


def forward_near_kernel(
    relay_ref, act_hbm, block_hbm, gains_hbm, bias_hbm, early_hbm, out_ref, early_ref,
    tail_ref, tail_gains_ref, once_ref, x_ref, gains_ref, bias_ref, sems, *refs
):
    relay = relay_ref[0]
    load_early = pltpu.make_async_copy(early_hbm, early_ref, sems.at[PIECES + 4])
    load_tail = pltpu.make_async_copy(block_hbm.at[block_hbm.shape[0] - TAIL :], tail_ref, sems.at[PIECES + 3])
    load_early.start()
    load_tail.start()
    loads, _ = arrive(
        act_hbm, None, x_ref, None, gains_hbm.at[relay], gains_ref, bias_hbm, bias_ref, sems
    )
    load_tail.wait()
    tail_gains_ref[...] = tail_ref[...].astype(F32)[:2]
    forward_section(x_ref, loads, gains_in(tail_gains_ref), bias_ref, once_ref, *refs)
    forward_section(once_ref, [], gains_in(gains_ref), bias_ref, out_ref, *refs)
    load_early.wait()


def forward_once_kernel(
    by_way_ref, direct_hbm, passed_hbm, far_hbm, bias_hbm, early_hbm, after, out_ref, early_ref, tail_ref, x_ref,
    gains_ref, bias_ref, sems, *refs
):
    load_early = pltpu.make_async_copy(early_hbm, early_ref, sems.at[PIECES + 3])
    load_early.start()
    direct = copies(direct_hbm, x_ref, sems)
    passed = copies(passed_hbm, x_ref, sems)

    @pl.when(by_way_ref[0] == 1)
    def _():
        start_all(passed)

    @pl.when(by_way_ref[0] == 0)
    def _():
        start_all(direct)

    tail = far_hbm.at[far_hbm.shape[0] - TAIL :]
    arrive(None, None, x_ref, None, tail, tail_ref, bias_hbm, bias_ref, sems)
    gains_ref[...] = tail_ref[...].astype(F32)[:2]
    forward_section(x_ref, direct, gains_in(gains_ref), bias_ref, out_ref, *refs)
    load_early.wait()


def forward_far_kernel(
    relay_ref, x_hbm, gains_hbm, bias_hbm, near_hbm, early_hbm, out_ref, early_ref, x_ref, gains_ref, bias_ref, sems, *refs
):
    relay = relay_ref[0]
    load_early = pltpu.make_async_copy(early_hbm, early_ref, sems.at[PIECES + 2])
    load_near = pltpu.make_async_copy(near_hbm, out_ref.at[1 - relay, 0, 0], sems.at[PIECES + 3])
    load_early.start()
    load_near.start()
    loads, _ = arrive(x_hbm, None, x_ref, None, gains_hbm.at[relay], gains_ref, bias_hbm, bias_ref, sems)
    forward_section(x_ref, loads, gains_in(gains_ref), bias_ref, out_ref.at[relay, 0, 0], *refs)
    load_near.wait()
    load_early.wait()


SMALL = pl.BlockSpec(memory_space=pltpu.SMEM)
NEAR = pl.BlockSpec(memory_space=pltpu.VMEM)
FAR = pl.BlockSpec(memory_space=pl.ANY)
PLAIN = pl.BlockSpec(memory_space=pltpu.HBM)


def call(kernel, name, operands, out_specs, out_shape, held, rows, width, kind, vmem=PART):
    block = pltpu.VMEM((rows, width), BF16)
    scratch = [block if h is None else h for h in held]
    if kind > 0:
        scratch += [
            pltpu.VMEM((2, width), F32),
            pltpu.VMEM((rows, rows), F32),
            pltpu.SemaphoreType.DMA((PIECES + 5,)),
            block,
            block,
            pltpu.VMEM((rows, width), F32),
            pltpu.VMEM((rows, HD), F32),
        ]
    if kind > 1:
        scratch += [pltpu.VMEM((rows, HD), F32), pltpu.VMEM((rows, HD), F32), block, block, pltpu.VMEM((rows, width), F32)]
    return pl.pallas_call(
        kernel,
        out_shape=out_shape,
        in_specs=[SMALL if x.dtype == jnp.int32 else PLAIN if x.ndim > 4 else FAR for x in operands],
        out_specs=out_specs,
        scratch_shapes=scratch,
        compiler_params=pltpu.CompilerParams(vmem_limit_bytes=vmem),
        cost_estimate=pl.CostEstimate(flops=0, bytes_accessed=COST, transcendentals=0),
        name=name,
    )(*operands)


def shape(*sizes, dtype=BF16):
    return jax.ShapeDtypeStruct(sizes, dtype)


def pick(relay, saved, act, own, mirrored):
    rows, width = act.shape[-2:]
    small = pltpu.VMEM((2, width), BF16)
    long = pltpu.VMEM((rows + TAIL, width), BF16)
    return call(
        pick_kernel, "pick", (relay, saved, act, own, mirrored), (FAR,) * 4,
        (shape(rows + TAIL, width), shape(rows, width)) * 2,
        [long, None, long, None, small, small, pltpu.SemaphoreType.DMA((10,))], rows, width, 0, FULL,
    )


def hold(way, small):
    return pl.pallas_call(
        hold_kernel,
        out_shape=(shape(*way.shape), shape(*small.shape, dtype=F32)),
        in_specs=[FAR, FAR],
        out_specs=(FAR, NEAR),
        scratch_shapes=[pltpu.SemaphoreType.DMA((1,))],
        input_output_aliases={0: 0},
        compiler_params=pltpu.CompilerParams(vmem_limit_bytes=MEBI),
        cost_estimate=pl.CostEstimate(flops=0, bytes_accessed=COST, transcendentals=0),
        name="hold",
    )(way, small)


def look(far, first):
    rows, width = far.shape
    return call(
        look_kernel, "look", (far, first), NEAR, shape(*first.shape, dtype=F32), [pltpu.SemaphoreType.DMA((1,))],
        rows, width, 0,
    )


def backward_first(x, dy, own, mirrored, bias):
    rows, width = x.shape[-2:]
    block = shape(rows, width)
    held = shape(2, width, dtype=F32)
    small = pltpu.VMEM((2, width), BF16)
    return call(
        backward_first_kernel, "backward_first", (x, dy, own, mirrored, bias), (NEAR,) * 5,
        (block, block, held, held, shape(2, 2, width, dtype=F32)),
        [small, small, None, None, pltpu.VMEM((2, width), F32), pltpu.SemaphoreType.DMA((3,)), None, None],
        rows, width, 2, MOST,
    )


def backward_next(choice, x, first, second, bias, after, also):
    rows, width = first.shape
    return call(
        backward_next_kernel, "backward_next", (choice, x, first, second, bias, after, also),
        NEAR, shape(2, width, dtype=F32), [pltpu.VMEM((TAIL, width), BF16), None, None], rows, width, 2,
    )


def forward_near(relay, act, tail, gains, bias, early):
    rows, width = act.shape
    return call(
        forward_near_kernel, "forward_near", (relay, act, tail, gains, bias, early), (NEAR, NEAR),
        (shape(rows, width), shape(*early.shape, dtype=F32)),
        [pltpu.VMEM((TAIL, width), BF16), pltpu.VMEM((2, width), F32), None, None], rows, width, 1,
    )


def forward_once(by_way, direct, passed, far, bias, early, after):
    rows, width = direct.shape
    return call(
        forward_once_kernel, "forward_once", (by_way, direct, passed, far, bias, early, after), (NEAR, NEAR),
        (shape(rows, width), shape(*early.shape, dtype=F32)), [pltpu.VMEM((TAIL, width), BF16), None], rows, width, 1,
    )


def forward_far(relay, x, gains, bias, near, early):
    rows, width = x.shape
    return call(
        forward_far_kernel, "forward_far", (relay, x, gains, bias, near, early), (NEAR, NEAR),
        (shape(2, 1, 1, rows, width), shape(*early.shape, dtype=F32)), [None], rows, width, 1,
    )


def summed_along(value, total, axis, stride, size):
    for step in range(1, size):
        pairs = []
        for i in range(lax.axis_size(axis)):
            place = i // stride % size
            pairs.append((i, i + ((place + step) % size - place) * stride))
        total = total + lax.ppermute(value, axis, pairs)
    return total


def routes(count):
    low, high, last = count // 2 - 1, count // 2, count - 1
    near = [(i, i ^ 1) for i in range(count)]
    far = [(i, i + 1) for i in range(1, last, 2) if i != low]
    far = far + [(b, a) for a, b in far]
    straight = [(low, high), (high, low)]
    out = [(low, 0), (high, last)]
    on = [(0, high), (last, low)]
    return near, far, straight, out, on


def body(act_in, grad_in, saved_inputs, first_key, norm_gains):
    rows = act_in.shape[3]
    count = lax.axis_size("section")
    last = count - 1
    near, far, straight, out, on = routes(count)
    mirror = [(i, last - i) for i in range(count)]
    section = lax.axis_index("section")
    odd = section % 2
    ends = (section == count // 2 - 1) | (section == count // 2)
    outer = jnp.stack([1 - odd]).astype(jnp.int32)
    inner = jnp.stack([odd]).astype(jnp.int32)
    by_way = jnp.stack([ends]).astype(jnp.int32)

    own = norm_gains[0]
    mirrored = lax.ppermute(own, "section", mirror)
    query = lax.broadcasted_iota(jnp.int32, (rows, rows), 0)
    key = lax.broadcasted_iota(jnp.int32, (rows, rows), 1)
    visible = (key <= query) & (key >= first_key[0][:, None])
    bias = jnp.where(visible, 0.0, HIDDEN).astype(F32)
    far_sent, act_sent, near_sent, near_act = pick(outer, saved_inputs, act_in, own, mirrored)
    far_block = lax.ppermute(far_sent, "section", far + straight)
    half_way = lax.ppermute(act_sent, "section", out)
    far_act = lax.ppermute(act_sent, "section", far)
    near_block = lax.ppermute(near_sent, "section", near)
    near_act = lax.ppermute(near_act, "section", near)

    dx_down, dx_up, first_down, first_up, gains = backward_first(saved_inputs, grad_in, own, mirrored, bias)
    half_way, first_up = hold(half_way, first_up)
    passed_act = lax.ppermute(half_way, "section", on)
    near_out, first_up = forward_near(outer, near_act, near_block, gains, bias, first_up)
    first_up = look(far_block, first_up)
    far_second = backward_next(inner, far_block, dx_down, dx_up, bias, first_up, first_up)
    near_second = backward_next(inner, near_block, dx_up, dx_down, bias, far_second, far_act)
    there = lax.ppermute(first_up, "section", mirror)
    down = jnp.where(odd == 1, near_second, far_second)
    up = jnp.where(odd == 1, far_second, near_second)
    down = lax.ppermute(down, "section", [(i, i - 1) for i in range(1, count)])
    up = lax.ppermute(up, "section", [(i, last - 1 - i) for i in range(last)])
    once, here = forward_once(by_way, far_act, passed_act, far_block, bias, first_down, near_second)
    total = here + there + down + up
    outputs, same = forward_far(inner, once, gains, bias, near_out, total)
    part = summed_along(total, same, "dp", 1, 4)
    combined = summed_along(part, part, "dp", 4, lax.axis_size("dp") // 4)
    return (outputs, combined[None])


def solution(mesh):
    placed = (
        P(None, "section", "dp", None, None),
        P(None, "section", "dp", None, None),
        P(None, None, "section", "dp", None, None),
        P("dp", None),
        P("section", None, None),
    )
    return jax.shard_map(
        body,
        mesh=mesh,
        in_specs=placed,
        out_specs=(P(None, "section", "dp", None, None), P("section", None, None)),
        check_vma=False,
    )
```
